256 devices in a mesh: row: 64 (over z, y, core), col: 4 (over x).
Axes of the slice: x: 4, y: 4, z: 8, core: 2. Of those that a mesh axis runs over, the one named last changes fastest.
Arguments:
- fine_latent: bfloat16 [98304, 512], P(('row', 'col')), may hold values from -6 to 6
- mid_latent: bfloat16 [8192, 512], P(('row', 'col')), may hold values from -6 to 6
- send_index: int32 [49152], P(('row', 'col')), may hold values from 0 to 383
- edge_src: int32 [589824], P(('row', 'col')), may hold values from 0 to 575
- edge_dst: int32 [589824], P(('row', 'col')), may hold values from 0 to 383
- edge_count: int32 [256], P(('row', 'col')), may hold values from 1152 to 2304, as said below
- up_row: int32 [98304, 1], P(('row', 'col')), may hold values from 0 to 63; in each aligned block of 384 rows (0 to 383, 384 to 767, ...) at most 12 rows name the same one
- up_node: int32 [98304], P(('row', 'col')), may hold values from 0 to 31
- w_src: bfloat16 [512, 512], replicated, may hold values from -0.25 to 0.25
- w_dst: bfloat16 [512, 512], replicated, may hold values from -0.25 to 0.25
- w_msg: bfloat16 [512, 512], replicated, may hold values from -0.25 to 0.25
- w_node: bfloat16 [1024, 512], replicated, may hold values from -0.1875 to 0.1875
- w_mid: bfloat16 [1024, 512], replicated, may hold values from -0.1875 to 0.1875
- cot_fine: bfloat16 [98304, 512], P(('row', 'col')), may hold values from -6 to 6
- cot_mid: bfloat16 [8192, 512], P(('row', 'col')), may hold values from -6 to 6
Outputs:
- fine_out: bfloat16 [98304, 512], P(('row', 'col'))
- mid_out: bfloat16 [8192, 512], P(('row', 'col'))
- grad_fine: bfloat16 [98304, 512], P(('row', 'col'))
- grad_mid: bfloat16 [8192, 512], P(('row', 'col'))
- weight_grads: float32 [1835008], P(('row', 'col'))
The draws below stay inside these ranges and needn't reach their ends.
Inputs may be any that keep to these rules, and one draw needn't show every extreme that they name: `up_row`: at most 12 of one device's fine nodes name the same row group, and some device reaches 12 in every draw. `edge_count`: some partition has all 2304 slots live in every draw.
All inputs are finite; a program needn't handle non-finite values.
Results may differ from the reference program's by a relative error of at most 0.023.
Values may be sent and summed in bfloat16 or wider, within the bound.
No kernel may reach another device: no remote copies, remote signals or barrier semaphores. Data moves between devices by JAX's collectives and lax.ppermute only.
A program may use at most 64 MiB of HBM per device.

```python
import math
import jax
import jax.numpy as jnp
import numpy as np
from jax import lax

D = 512
NF_DEV = 384
NM_DEV = 32
HALO = 96
E_DEV = 2304
CAP = 12
DEVS = 256
FINE = 98304
MID = 8192
EDGES = 589824
SENDS = 49152
N_ROW = 64
N_COL = 4


def draw_edge_count(key, part):
    key = jax.random.fold_in(key, 7)
    first_key, second_key = jax.random.split(key)
    values = jax.random.randint(first_key, (DEVS,), E_DEV // 2, E_DEV + 1)
    spot = jax.random.randint(second_key, (), 0, DEVS)
    return values.at[spot].set(E_DEV).astype(jnp.int32)


def plant(drawn, rng, smallest, largest):
    longest = drawn.shape.index(max(drawn.shape))
    spots = []
    for shift in (0, 1):
        where = [jax.random.randint(jax.random.fold_in(rng, axis), (), 0, length) for axis, length in enumerate(drawn.shape)]
        where[longest] = (where[longest] + shift) % drawn.shape[longest]
        spots.append(tuple(where))
    return drawn.at[spots[0]].set(smallest).at[spots[1]].set(largest)


def block_scale(rng, dims, pieces, least, high):
    def one(dim, blocks):
        steps = jax.random.uniform(jax.random.fold_in(jax.random.fold_in(rng, 6), dim), (blocks,), jnp.float32, least / len(pieces), high / len(pieces))
        return jnp.repeat(jnp.exp(steps), dims[dim] // blocks).reshape((-1,) + (1,) * (len(dims) - dim - 1))

    level = one(*pieces[0])
    for cut in pieces[1:]:
        level = level * one(*cut)
    return level


def deal_out(own_key, own, number, rows, count, top, limit, lean):
    ranking = jax.random.permutation(own_key, count)
    crowded, common = load_shares(count, rows * top, limit, lean, True), load_shares(count, rows * top, limit, lean, False)
    places = jnp.arange(count)

    def named(lengths, rotation):
        used = int((lengths > 0).sum())
        fixed = max(1, used // 4)
        shifted = fixed + (places - fixed + rotation * (used - fixed)) % max(1, count - fixed)
        return jnp.zeros((count,), jnp.int32).at[ranking[jnp.where(places < fixed, places, shifted)]].set(jnp.asarray(lengths, jnp.int32))

    lengths = jnp.where(number % 4 == 0, named(crowded, number // 4), named(common, number - number // 4 - 1))
    mixed = jax.random.permutation(jax.random.fold_in(own, 3), count)
    donor, taker = mixed[0:count // 2 * 2:2], mixed[1:count // 2 * 2:2]
    margin = jnp.minimum(lengths[donor] - 1, limit - lengths[taker]) // 2
    margin = jnp.where((donor == ranking[0]) | (taker == ranking[0]) | (lengths[taker] == 0), 0, jnp.maximum(margin, 0))
    shifted = jax.random.randint(jax.random.fold_in(own, 4), (count // 2,), 0, 1 << 20) % (margin + 1)
    lengths = lengths.at[donor].add(-shifted).at[taker].add(shifted)
    members = jnp.searchsorted(jnp.cumsum(lengths), jnp.arange(rows * top), side="right").astype(jnp.int32)
    listing = members.reshape(top, rows).T
    listing = listing[jax.random.permutation(jax.random.fold_in(own, 1), rows)]
    rotation = jax.random.randint(jax.random.fold_in(own, 2), (rows, 1), 0, top)
    return jnp.take_along_axis(listing, (jnp.arange(top)[None, :] + rotation) % top, axis=1)


def load_shares(number_of, total, most, slope, full):
    portions = [(1 << 20) // math.isqrt(standing ** slope) + 1 for standing in range(1, number_of + 1)]
    largest = most if full else min(most, max(-(-total // number_of), total * portions[0] // sum(portions)))
    least = 1 if total - largest >= number_of - 1 else 0
    counts, rest = [largest] + [least] * (number_of - 1), total - largest - least * (number_of - 1)
    while rest > 0:
        free = [i for i in range(1, number_of) if counts[i] < largest] or [i for i in range(1, number_of) if counts[i] < most]
        mass, remaining = sum([portions[i] for i in free]), rest
        for i in free:
            addition = min(most - counts[i], max(1, remaining * portions[i] // mass), rest)
            counts[i] = counts[i] + addition
            rest = rest - addition
    return np.array(counts)


def centred(key, dims, scale, limit, cuts=(), held_as=jnp.bfloat16):
    entries = scale * jax.random.normal(key, dims, jnp.float32)
    if cuts:
        entries = entries * block_scale(key, dims, cuts, -0.22, 0.18)
    return jnp.clip(entries, -limit, limit).astype(held_as)


def setup_inputs(seed: int = 0) -> dict:
    keys = jax.random.split(jax.random.key(seed), 16)
    fine_latent = centred(keys[0], (FINE, D), 1.0, 6.0, ((0, 256),))
    mid_latent = centred(keys[1], (MID, D), 1.0, 6.0, ((0, 256),))
    send_index = plant(jax.random.randint(keys[2], (SENDS,), 0, NF_DEV), jax.random.fold_in(keys[2], 1), 0, NF_DEV - 1).astype(jnp.int32)
    edge_src = plant(jax.random.randint(keys[3], (EDGES,), 0, NF_DEV + 2 * HALO), jax.random.fold_in(keys[3], 1), 0, (NF_DEV + 2 * HALO) - 1).astype(jnp.int32)
    edge_dst = plant(jax.random.randint(keys[4], (EDGES,), 0, NF_DEV), jax.random.fold_in(keys[4], 1), 0, NF_DEV - 1).astype(jnp.int32)
    edge_count = draw_edge_count(jax.random.fold_in(keys[15], 71), 0)
    up_row_keys = jax.random.split(jax.random.fold_in(keys[6], 1), FINE // NF_DEV)
    up_row_turns = jax.random.permutation(jax.random.fold_in(keys[6], 3), FINE // NF_DEV)
    up_row = jax.vmap(lambda own, number: deal_out(jax.random.fold_in(keys[6], 2), own, number, NF_DEV, N_ROW, 1, CAP, 2))(up_row_keys, up_row_turns).reshape((FINE, 1))
    up_node = plant(jax.random.randint(keys[7], (FINE,), 0, NM_DEV), jax.random.fold_in(keys[7], 1), 0, NM_DEV - 1).astype(jnp.int32)
    w_src = centred(keys[8], (D, D), D ** -0.5, 0.25)
    w_dst = centred(keys[9], (D, D), D ** -0.5, 0.25)
    w_msg = centred(keys[10], (D, D), D ** -0.5, 0.25)
    w_node = centred(keys[11], (2 * D, D), (2 * D) ** -0.5, 0.1875)
    w_mid = centred(keys[12], (2 * D, D), (2 * D) ** -0.5, 0.1875)
    cot_fine = centred(keys[13], (FINE, D), 1.0, 6.0, ((0, 256),))
    cot_mid = centred(keys[14], (MID, D), 1.0, 6.0, ((0, 256),))
    return dict(fine_latent=fine_latent, mid_latent=mid_latent, send_index=send_index, edge_src=edge_src, edge_dst=edge_dst, edge_count=edge_count, up_row=up_row, up_node=up_node, w_src=w_src, w_dst=w_dst, w_msg=w_msg, w_node=w_node, w_mid=w_mid, cot_fine=cot_fine, cot_mid=cot_mid)


def fine_part(latent, lower_rim, upper_rim, sources, targets, live_count, w_src, w_dst, w_msg, w_node):
    extended = jnp.concatenate([latent, lower_rim, upper_rim], axis=0)
    proj_src = jnp.dot(extended, w_src, preferred_element_type=jnp.float32).astype(jnp.bfloat16)
    proj_dst = jnp.dot(latent, w_dst, preferred_element_type=jnp.float32).astype(jnp.bfloat16)
    preact = proj_src[sources].astype(jnp.float32) + proj_dst[targets].astype(jnp.float32)
    edge_live = jnp.arange(sources.shape[0], dtype=jnp.int32) < live_count
    activity = jnp.where(edge_live[:, None], jax.nn.silu(preact), 0.0).astype(jnp.bfloat16)
    message = jnp.dot(activity, w_msg, preferred_element_type=jnp.float32).astype(jnp.bfloat16)
    onehot = (targets[:, None] == jnp.arange(latent.shape[0], dtype=jnp.int32)[None, :]).astype(jnp.bfloat16)
    aggregate = lax.dot_general(onehot, message, (((0,), (0,)), ((), ())), preferred_element_type=jnp.float32).astype(jnp.bfloat16)
    joined = jnp.concatenate([latent, aggregate], axis=1)
    update = jnp.dot(joined, w_node, preferred_element_type=jnp.float32)
    return (latent.astype(jnp.float32) + jax.nn.silu(update)).astype(jnp.bfloat16)

def mid_part(mid_block, mid_total, w_mid):
    up_agg = (0.25 * mid_total).astype(jnp.bfloat16)
    joined = jnp.concatenate([mid_block, up_agg], axis=1)
    update = jnp.dot(joined, w_mid, preferred_element_type=jnp.float32)
    return (mid_block.astype(jnp.float32) + jax.nn.silu(update)).astype(jnp.bfloat16)

def reference(fine_latent, mid_latent, send_index, edge_src, edge_dst, edge_count, up_row, up_node, w_src, w_dst, w_msg, w_node, w_mid, cot_fine, cot_mid):
    device_count = N_ROW * N_COL
    latent_blocks = fine_latent.reshape(device_count, NF_DEV, D)
    send_blocks = send_index.reshape(device_count, 2 * HALO)
    send_rows = jax.vmap(lambda block, places: block[places])(latent_blocks, send_blocks)
    lower_rims = jnp.roll(send_rows[:, HALO:], 1, axis=0)
    upper_rims = jnp.roll(send_rows[:, :HALO], -1, axis=0)
    source_blocks = edge_src.reshape(device_count, E_DEV)
    target_blocks = edge_dst.reshape(device_count, E_DEV)

    def forward_one(items):
        latent, lower_rim, upper_rim, sources, targets, live_count = items
        return fine_part(latent, lower_rim, upper_rim, sources, targets, live_count, w_src, w_dst, w_msg, w_node)
    fine_new = lax.map(forward_one, (latent_blocks, lower_rims, upper_rims, source_blocks, target_blocks, edge_count))
    column = jnp.arange(device_count, dtype=jnp.int32) % N_COL
    parent = (up_row.reshape(device_count, NF_DEV) * N_COL + column[:, None]) * NM_DEV + up_node.reshape(device_count, NF_DEV)
    parent = parent.reshape(-1).astype(jnp.int32)
    mid_total = jax.ops.segment_sum(fine_new.reshape(-1, D).astype(jnp.float32), parent, num_segments=device_count * NM_DEV)

    def mid_step(running, items):
        mid_block, total_block, cot_block = items
        result, back = jax.vjp(mid_part, mid_block, total_block, w_mid)
        grad_block, grad_total, grad_weight = back(cot_block)
        return (running + grad_weight.astype(jnp.float32), (result, grad_block, grad_total))
    mid_running, (mid_new, mid_grads, total_grads) = lax.scan(mid_step, jnp.zeros((2 * D, D), jnp.float32), (mid_latent.reshape(device_count, NM_DEV, D), mid_total.reshape(device_count, NM_DEV, D), cot_mid.reshape(device_count, NM_DEV, D)))
    up_grad = total_grads.reshape(-1, D)[parent].astype(jnp.bfloat16)
    fine_cot = (cot_fine.astype(jnp.float32) + up_grad.astype(jnp.float32)).astype(jnp.bfloat16)

    def fine_step(running, items):
        latent, lower_rim, upper_rim, sources, targets, live_count, grad_out = items

        def closure(first, second, third, ws, wd, wm, wn):
            return fine_part(first, second, third, sources, targets, live_count, ws, wd, wm, wn)
        _, back = jax.vjp(closure, latent, lower_rim, upper_rim, w_src, w_dst, w_msg, w_node)
        grads = back(grad_out)
        running = tuple((total + piece.astype(jnp.float32) for total, piece in zip(running, grads[3:])))
        return (running, grads[:3])
    start = (jnp.zeros((D, D), jnp.float32), jnp.zeros((D, D), jnp.float32), jnp.zeros((D, D), jnp.float32), jnp.zeros((2 * D, D), jnp.float32))
    fine_running, (grad_latent, grad_lower, grad_upper) = lax.scan(fine_step, start, (latent_blocks, lower_rims, upper_rims, source_blocks, target_blocks, edge_count, fine_cot.reshape(device_count, NF_DEV, D)))
    send_grads = jnp.concatenate([jnp.roll(grad_upper, 1, axis=0), jnp.roll(grad_lower, -1, axis=0)], axis=1)
    grad_fine = jax.vmap(lambda base, places, values: base.at[places].add(values))(grad_latent.astype(jnp.float32), send_blocks, send_grads.astype(jnp.float32)).astype(jnp.bfloat16)
    weight_grads = jnp.concatenate([piece.reshape(-1) for piece in fine_running + (mid_running,)])
    return (fine_new.reshape(-1, D), mid_new.reshape(-1, D), grad_fine.reshape(-1, D), mid_grads.reshape(-1, D), weight_grads)
```

```python
import jax
import jax.numpy as jnp
from jax import lax
from jax.sharding import PartitionSpec as P

BF = jnp.bfloat16
F32 = jnp.float32
BOTH = ("row", "col")
CAP = 12
ZN, YN, CN, XN = 8, 4, 2, 4
PLANE = YN * CN


def place(z, y, c, x):
    return ((z * YN + y) * CN + c) * XN + x


def shift(dz=0, dy=0, dc=0, dx=0):
    return [
        (place(z, y, c, x), place((z + dz) % ZN, (y + dy) % YN, (c + dc) % CN, (x + dx) % XN))
        for z in range(ZN)
        for y in range(YN)
        for c in range(CN)
        for x in range(XN)
    ]


PLANES = [[z * PLANE + i for i in range(PLANE)] for z in range(ZN)]
PILLARS = [[z * PLANE + i for z in range(ZN)] for i in range(PLANE)]


def dot(a, b):
    return jnp.dot(a, b, preferred_element_type=F32)


def dot_t(a, b):
    return lax.dot_general(a, b, (((0,), (0,)), ((), ())), preferred_element_type=F32)


def dot_nt(a, b):
    return lax.dot_general(a, b, (((1,), (1,)), ((), ())), preferred_element_type=F32)


def one_hot(index, count):
    return (index[:, None] == jnp.arange(count, dtype=jnp.int32)[None, :]).astype(BF)


def pick(block, index, axis):
    return lax.dynamic_index_in_dim(block, index, axis, keepdims=False)


def silu_pair(u):
    s = jax.nn.sigmoid(u)
    return u * s, s * (1.0 + u * (1.0 - s))


def reduce_weights(flat):
    row = lax.axis_index("row")
    core, yy, xx = row % CN, (row // CN) % YN, lax.axis_index("col")
    cut = flat.astype(BF).reshape(ZN * YN, CN, XN * 14, 512)
    got = lax.ppermute(pick(cut, 1 - core, 1), BOTH, shift(dc=1))
    part = (pick(cut, core, 1).astype(F32) + got.astype(F32)).astype(BF)
    part = part.reshape(ZN * YN, XN, 14, 512)
    terms = [pick(part, xx, 1)]
    for d in (1, 3, 2):
        terms.append(lax.ppermute(pick(part, (xx + d) % XN, 1), BOTH, shift(dx=d)))
    part = sum(t.astype(F32) for t in terms).astype(BF).reshape(ZN, YN, 14, 512)
    terms = [pick(part, yy, 1)]
    for d in (1, 3, 2):
        terms.append(lax.ppermute(pick(part, (yy + d) % YN, 1), BOTH, shift(dy=d)))
    part = sum(t.astype(F32) for t in terms).astype(BF)
    got = lax.all_to_all(part, "row", 0, 0, axis_index_groups=PILLARS)
    return jnp.sum(got.astype(F32), axis=0).reshape(-1)


def on_device(
    fine_latent,
    mid_latent,
    send_index,
    edge_src,
    edge_dst,
    edge_count,
    up_row,
    up_node,
    w_src,
    w_dst,
    w_msg,
    w_node,
    w_mid,
    cot_fine,
    cot_mid,
):
    nodes, width = fine_latent.shape
    rim = send_index.shape[0] // 2
    mids = mid_latent.shape[0]
    row = lax.axis_index("row")

    pick_send = one_hot(send_index, nodes)
    send_rows = dot(pick_send, fine_latent).astype(BF)
    ahead = [(i, (i + 1) % 256) for i in range(256)]
    behind = [(j, i) for i, j in ahead]
    lower_rim = lax.ppermute(send_rows[rim:], BOTH, ahead)
    upper_rim = lax.ppermute(send_rows[:rim], BOTH, behind)

    dest = up_row[:, 0]
    same = dest[:, None] == dest[None, :]
    earlier = jnp.arange(nodes)[None, :] < jnp.arange(nodes)[:, None]
    rank = jnp.sum((same & earlier).astype(jnp.int32), axis=1)
    spot = (dest % PLANE) * (ZN * CAP) + (dest // PLANE) * CAP + rank
    slots = PLANE * ZN * CAP
    to_slot = one_hot(spot, slots)
    names = dot_t(to_slot, (up_node + 1).astype(BF)[:, None])[:, 0].astype(jnp.int32) - 1
    names = lax.all_gather(
        names.reshape(PLANE, ZN * CAP), "row", axis_index_groups=PLANES
    )
    names = pick(names, row % PLANE, 1)
    level = (jnp.arange(ZN * CAP, dtype=jnp.int32) // CAP * mids)[None, :]
    owner = jnp.where(names >= 0, names + level, -1).reshape(-1)
    to_mid = one_hot(owner, ZN * mids)

    extended = jnp.concatenate([fine_latent, lower_rim, upper_rim], axis=0)
    proj_src = dot(extended, w_src).astype(BF)
    proj_dst = dot(fine_latent, w_dst).astype(BF)
    ends = jnp.concatenate(
        [one_hot(edge_src, extended.shape[0]), one_hot(edge_dst, nodes)], axis=1
    )
    preact = dot(ends, jnp.concatenate([proj_src, proj_dst], axis=0))
    live = (jnp.arange(edge_src.shape[0], dtype=jnp.int32) < edge_count[0])[:, None]
    act, slope = silu_pair(preact)
    act = jnp.where(live, act, 0.0).astype(BF)
    slope = jnp.where(live, slope, 0.0).astype(BF)
    pick_dst = one_hot(edge_dst, nodes)
    gathered = dot_t(pick_dst, act).astype(BF)
    aggregate = dot(gathered, w_msg).astype(BF)
    joined = jnp.concatenate([fine_latent, aggregate], axis=1)
    lift, node_slope = silu_pair(dot(joined, w_node))
    fine_out = (fine_latent.astype(F32) + lift).astype(BF)

    sent = dot_t(to_slot, fine_out).astype(BF).reshape(PLANE, ZN * CAP, width)
    got = lax.all_to_all(sent, "row", 0, 0, axis_index_groups=PLANES).reshape(slots, width)
    sums = dot_t(to_mid, got).astype(BF).reshape(ZN, mids, width)
    sums = lax.all_to_all(sums, "row", 0, 0, axis_index_groups=PILLARS)
    mid_total = jnp.sum(sums.astype(F32), axis=0)
    up_agg = (0.25 * mid_total).astype(BF)
    mid_joined = jnp.concatenate([mid_latent, up_agg], axis=1)
    mid_lift, mid_slope = silu_pair(dot(mid_joined, w_mid))
    mid_out = (mid_latent.astype(F32) + mid_lift).astype(BF)
    mid_back = (cot_mid.astype(F32) * mid_slope).astype(BF)
    grad_joined = dot_nt(mid_back, w_mid).astype(BF)
    grad_mid = (cot_mid.astype(F32) + grad_joined[:, :width].astype(F32)).astype(BF)
    grad_total = (0.25 * grad_joined[:, width:].astype(F32)).astype(BF)
    grad_wmid = dot_t(mid_joined, mid_back)

    spread = jnp.broadcast_to(grad_total[None], (ZN, mids, width))
    spread = lax.all_to_all(spread, "row", 0, 0, axis_index_groups=PILLARS)
    back = dot(to_mid, spread.reshape(ZN * mids, width)).astype(BF)
    back = lax.all_to_all(
        back.reshape(PLANE, ZN * CAP, width), "row", 0, 0, axis_index_groups=PLANES
    )
    up_grad = dot(to_slot, back.reshape(slots, width))
    fine_cot = (cot_fine.astype(F32) + up_grad).astype(BF)

    node_back = (fine_cot.astype(F32) * node_slope).astype(BF)
    grad_node = dot_nt(node_back, w_node).astype(BF)
    grad_wnode = dot_t(joined, node_back)
    grad_agg = grad_node[:, width:]
    grad_wmsg = dot_t(gathered, grad_agg)
    grad_gathered = dot_nt(grad_agg, w_msg).astype(BF)
    grad_edge = (dot(pick_dst, grad_gathered) * slope.astype(F32)).astype(BF)
    grad_ends = dot_t(ends, grad_edge).astype(BF)
    grad_src, grad_dst = grad_ends[: extended.shape[0]], grad_ends[extended.shape[0] :]
    grad_wsrc = dot_t(extended, grad_src)
    grad_wdst = dot_t(fine_latent, grad_dst)
    grad_ext = dot_nt(grad_src, w_src)
    rims = grad_ext[nodes:].astype(BF)
    from_low = lax.ppermute(rims[rim:], BOTH, ahead)
    from_high = lax.ppermute(rims[:rim], BOTH, behind)
    direct = (
        fine_cot.astype(F32)
        + grad_node[:, :width].astype(F32)
        + grad_ext[:nodes]
        + dot_nt(grad_dst, w_dst)
    )
    returned = dot_t(pick_send, jnp.concatenate([from_low, from_high], axis=0))
    grad_fine = (direct + returned).astype(BF)

    flat = jnp.concatenate([grad_wsrc, grad_wdst, grad_wmsg, grad_wnode, grad_wmid], axis=0)
    return fine_out, mid_out, grad_fine, grad_mid, reduce_weights(flat)


def solution(mesh):
    rows, line = P(BOTH, None), P(BOTH)
    return jax.shard_map(
        on_device,
        mesh=mesh,
        in_specs=(rows, rows, line, line, line, line, rows, line)
        + (P(),) * 5
        + (rows, rows),
        out_specs=(rows, rows, rows, rows, line),
        check_vma=False,
    )
```

```python
import jax
import jax.numpy as jnp
from jax import lax
from jax.experimental import pallas as pl
from jax.experimental.pallas import tpu as pltpu
from jax.sharding import PartitionSpec as P

BF = jnp.bfloat16
F32 = jnp.float32
BOTH = ("row", "col")
CAP = 12
ZN, YN, CN, XN = 8, 4, 2, 4
PLANE = YN * CN
NODES, RIM, EXT, MIDS, WIDTH, EDGES = 384, 96, 576, 32, 512, 2304
SLOTS = ZN * CAP
CARRY = 112
STEP = 768
DST = 640
ENDS = DST + NODES
TALL = 14
HELD = 16


def place(z, y, c, x):
    return ((z * YN + y) * CN + c) * XN + x


def shift(dz=0, dy=0, dc=0, dx=0):
    return [
        (place(z, y, c, x), place((z + dz) % ZN, (y + dy) % YN, (c + dc) % CN, (x + dx) % XN))
        for z in range(ZN)
        for y in range(YN)
        for c in range(CN)
        for x in range(XN)
    ]


PLANES = [[z * PLANE + i for i in range(PLANE)] for z in range(ZN)]
PILLARS = [[z * PLANE + i for z in range(ZN)] for i in range(PLANE)]
SHEETS = [
    [place(z, y, c, x) for y in range(YN) for x in range(XN)] for z in range(ZN) for c in range(CN)
]


def dot(a, b):
    return jnp.dot(a, b, preferred_element_type=F32)


def dot_t(a, b):
    return lax.dot_general(a, b, (((0,), (0,)), ((), ())), preferred_element_type=F32)


def dot_nt(a, b):
    return lax.dot_general(a, b, (((1,), (1,)), ((), ())), preferred_element_type=F32)


def iota(shape, axis):
    return lax.broadcasted_iota(jnp.int32, shape, axis)


def ones(mask):
    return jnp.where(mask, 1.0, 0.0).astype(BF)


def across(row):
    return jnp.transpose(jnp.broadcast_to(row, (128, 128)))


def down(row, count, start=0):
    return ones(iota((count, row.shape[1]), 0) + start == row)


def silu_pair(u):
    s = 0.5 * jnp.tanh(0.5 * u) + 0.5
    return u * s, s * (1.0 + u * (1.0 - s))


def bf(*shape):
    return jax.ShapeDtypeStruct(shape, BF)


def f32(*shape):
    return jax.ShapeDtypeStruct(shape, F32)


def i32(*shape):
    return jax.ShapeDtypeStruct(shape, jnp.int32)


def run(body, outs, args, kinds, scratch=(), copies=0, mib=16, flops=0):
    spaces = {"s": pltpu.SMEM, "v": pltpu.VMEM, "h": pltpu.HBM}
    moved = sum(a.size * a.dtype.itemsize for a in list(args) + list(outs))
    took, gave = kinds.split(">")
    scratch = list(scratch)
    if copies:
        scratch.append(pltpu.SemaphoreType.DMA((copies,)))
    return pl.pallas_call(
        body,
        out_shape=list(outs),
        in_specs=[pl.BlockSpec(memory_space=spaces[k]) for k in took],
        out_specs=[pl.BlockSpec(memory_space=spaces[k]) for k in gave],
        scratch_shapes=scratch,
        compiler_params=pltpu.CompilerParams(vmem_limit_bytes=mib << 20),
        cost_estimate=pl.CostEstimate(flops=flops, bytes_accessed=moved, transcendentals=0),
    )(*args)


def fetch(sems, *pairs):
    copies = [pltpu.make_async_copy(a, b, sems.at[i]) for i, (a, b) in enumerate(pairs)]
    for copy in copies:
        copy.start()
    return copies


def piece(line, start, size):
    return line[pl.ds(start, size)].reshape(1, size)


def send_body(index_far, latent_far, low, high, index, latent, sems):
    for copy in fetch(sems, (index_far, index), (latent_far, latent)):
        copy.wait()
    row = jnp.concatenate([piece(index, 0, 128), piece(index, 128, 64)], axis=1)
    rows = dot_t(down(row, NODES), latent[...]).astype(BF)
    low[...] = rows[:RIM]
    high[...] = rows[RIM:]


def local_body(
    dest_far, latent_far, w_src_far, w_dst_far, near, mine, spot, dest, latent, w_src, w_dst, sems
):
    copies = fetch(
        sems, (dest_far, dest), (latent_far, latent), (w_src_far, w_src), (w_dst_far, w_dst)
    )
    copies[0].wait()
    for j in range(NODES // 128):
        row = dest[:, 128 * j : 128 * (j + 1)]
        rank = jnp.zeros((1, 128), F32)
        for b in range(j + 1):
            same = across(dest[:, 128 * b : 128 * (b + 1)]) == row
            if b == j:
                same = same & (iota((128, 128), 0) < iota((128, 128), 1))
            rank = rank + jnp.sum(jnp.where(same, 1.0, 0.0), axis=0, keepdims=True)
        spot[:, 128 * j : 128 * (j + 1)] = (
            (row & (PLANE - 1)) * SLOTS + (row >> 3) * CAP + rank.astype(jnp.int32)
        )
    for copy in copies[1:]:
        copy.wait()
    near[...] = dot(latent[...], w_src[...]).astype(BF)
    mine[...] = dot(latent[...], w_dst[...]).astype(BF)


def live_row(row, count, start):
    return jnp.where(iota(row.shape, 1) + start < count, row, -1)


def forward_body(
    count,
    src_far,
    dst_far,
    near_far,
    mine_far,
    w_src_far,
    lower_far,
    upper_far,
    w_msg_far,
    w_node_far,
    latent_far,
    spot_far,
    node_far,
    fine_out_far,
    sent_far,
    node_slope_far,
    slope_far,
    gathered_far,
    aggregate_far,
    src,
    dst,
    mine,
    w_src,
    lower,
    upper,
    w_msg,
    w_node,
    latent,
    spot,
    node,
    fine_out,
    sent,
    node_slope,
    edge_slope,
    gathered,
    aggregate,
    table,
    ends,
    sems,
    out_sems,
):
    near = table.at[:NODES, :]
    copies = fetch(
        sems,
        (src_far, src),
        (dst_far, dst),
        (w_src_far, w_src),
        (lower_far, lower),
        (upper_far, upper),
        (near_far, near),
        (mine_far, mine),
        (w_msg_far, w_msg),
        (w_node_far, w_node),
        (latent_far, latent),
        (spot_far, spot),
        (node_far, node),
    )
    stores = []

    def store(here, there):
        stores.append(pltpu.make_async_copy(here, there, out_sems.at[len(stores)]))
        stores[-1].start()

    table[EXT:DST, :] = jnp.zeros((DST - EXT, WIDTH), BF)
    for copy in copies[:7]:
        copy.wait()
    table[DST:, :] = mine[...]
    table[NODES : NODES + RIM, :] = dot(lower[...], w_src[...]).astype(BF)
    table[NODES + RIM : EXT, :] = dot(upper[...], w_src[...]).astype(BF)
    lane = iota((128, 128), 1)
    total = jnp.zeros((NODES, WIDTH), F32)
    for start in range(0, EDGES, STEP):
        for at in range(start, start + STEP, 128):
            source, target = across(piece(src, at, 128)), across(piece(dst, at, 128))
            for j in range(0, DST, 128):
                ends[at : at + 128, j : j + 128] = ones(source == lane + j)
            for j in range(0, NODES, 128):
                ends[at : at + 128, DST + j : DST + j + 128] = ones(target == lane + j)
        act, slope = silu_pair(dot(ends[start : start + STEP, :], table[...]))
        here = pl.ds(start, STEP)
        edge_slope[here, :] = slope.astype(BF)
        store(edge_slope.at[here, :], slope_far.at[here, :])
        row = live_row(piece(dst, start, STEP), count[0], start)
        total = total + dot(down(row, NODES), act.astype(BF))
    gathered[...] = total.astype(BF)
    store(gathered, gathered_far)
    for copy in copies[7:]:
        copy.wait()
    aggregate[...] = dot(gathered[...], w_msg[...]).astype(BF)
    store(aggregate, aggregate_far)
    update = dot(latent[...], w_node[:WIDTH, :]) + dot(aggregate[...], w_node[WIDTH:, :])
    lift, slope = silu_pair(update)
    node_slope[...] = slope
    store(node_slope, node_slope_far)
    fine_out[...] = (latent[...].astype(F32) + lift).astype(BF)
    store(fine_out, fine_out_far)
    names = jnp.broadcast_to((piece(node, 0, NODES) + 1).astype(F32), (16, NODES)).astype(BF)
    for i in range(PLANE):
        offset = spot[...] - i * SLOTS
        to_slot = ones((iota((128, NODES), 0) == offset) & (offset < SLOTS))
        sent[i] = dot(to_slot[:CARRY], fine_out[...]).astype(BF)
        sent[i, SLOTS:CARRY, :128] = dot_nt(names, to_slot).astype(BF)
        if i % 4 == 3:
            store(sent.at[pl.ds(i - 3, 4)], sent_far.at[pl.ds(i - 3, 4)])
    for copy in stores:
        copy.wait()


def sum_body(got, sums, owner):
    total = jnp.zeros((ZN * MIDS, WIDTH), F32)
    level = iota((1, 128), 1)
    base = jnp.zeros((1, 128), jnp.int32)
    for z in range(1, ZN):
        base = base + jnp.where(level >= z * CAP, MIDS, 0)
    for i in range(PLANE):
        name = got[i, SLOTS:CARRY, :128][:1].astype(F32).astype(jnp.int32)
        name = jnp.where((name > 0) & (level < SLOTS), name - 1 + base, -1)
        owner[i : i + 1, :] = name
        total = total + dot(down(name, ZN * MIDS)[:, :CARRY], got[i])
    for z in range(ZN):
        sums[z] = total[z * MIDS : (z + 1) * MIDS].astype(BF)


def mid_body(
    got,
    latent_far,
    cot_far,
    w_mid_far,
    mid_out,
    grad_mid,
    spread,
    up_agg,
    mid_back,
    latent,
    cot,
    w_mid,
    sems,
):
    copies = fetch(sems, (latent_far, latent), (cot_far, cot), (w_mid_far, w_mid))
    total = got[0].astype(F32)
    for z in range(1, ZN):
        total = total + got[z].astype(F32)
    agg = (0.25 * total).astype(BF)
    up_agg[...] = agg
    for copy in copies:
        copy.wait()
    update = dot(latent[...], w_mid[:WIDTH, :]) + dot(agg, w_mid[WIDTH:, :])
    lift, slope = silu_pair(update)
    mid_out[...] = (latent[...].astype(F32) + lift).astype(BF)
    back = (cot[...].astype(F32) * slope).astype(BF)
    mid_back[...] = back
    grad = dot_nt(back, w_mid[:WIDTH, :]).astype(BF).astype(F32)
    grad_mid[...] = (cot[...].astype(F32) + grad).astype(BF)
    grad = dot_nt(back, w_mid[WIDTH:, :]).astype(BF).astype(F32)
    grad = (0.25 * grad).astype(BF)
    for z in range(ZN):
        spread[z] = grad


def spread_body(owner, got, back):
    rows = jnp.concatenate([got[z] for z in range(ZN)], axis=0)
    for i in range(PLANE):
        back[i] = dot_t(down(owner[i : i + 1, :], ZN * MIDS), rows)[:SLOTS].astype(BF)


def part_cores(flat, first, pairs, stage):
    for pair in range(first, first + pairs):
        for c in range(CN):
            rows = [flat[pl.ds(224 * pair + 112 * h + 56 * c, 56), :] for h in range(2)]
            rows = jnp.concatenate(rows, axis=0).astype(BF)
            stage[c, 112 * pair : 112 * (pair + 1), :] = rows


def backward_body(
    count,
    core,
    spot_far,
    back_far,
    cot_far,
    node_slope_far,
    w_node_far,
    w_msg_far,
    dst_far,
    gathered_far,
    latent_far,
    aggregate_far,
    mid_far,
    mid_back_far,
    up_agg_far,
    src_far,
    slope_far,
    lower_far,
    upper_far,
    w_src_far,
    w_dst_far,
    direct_far,
    low_far,
    high_far,
    keep_far,
    send_far,
    spot,
    back,
    cot,
    node_slope,
    w_node,
    w_msg,
    dst,
    gathered,
    latent,
    aggregate,
    mid,
    mid_back,
    up_agg,
    src,
    edge_slope,
    lower,
    upper,
    w_src,
    w_dst,
    node_back,
    grad_agg,
    grad_gathered,
    grad_ends,
    rims,
    direct,
    targets,
    total,
    flat,
    stage,
    sems,
    out_sems,
):
    copies = fetch(
        sems,
        (spot_far, spot),
        (back_far, back),
        (cot_far, cot),
        (node_slope_far, node_slope),
        (w_node_far, w_node),
        (w_msg_far, w_msg),
        (dst_far, dst),
        (gathered_far, gathered),
        (latent_far, latent),
        (aggregate_far, aggregate),
        (mid_far, mid),
        (mid_back_far, mid_back),
        (up_agg_far, up_agg),
        (src_far, src),
        (slope_far, edge_slope),
        (lower_far, lower),
        (upper_far, upper),
        (w_src_far, w_src),
        (w_dst_far, w_dst),
    )
    stores = []

    def store(here, there):
        stores.append(pltpu.make_async_copy(here, there, out_sems.at[len(stores)]))
        stores[-1].start()

    mine = core[0]
    for copy in copies[:2]:
        copy.wait()
    up = jnp.zeros((NODES, WIDTH), F32)
    for i in range(PLANE):
        up = up + dot_t(down(spot[...], SLOTS, i * SLOTS), back[i])
    for copy in copies[2:4]:
        copy.wait()
    cot_sum = (cot[...].astype(F32) + up).astype(BF).astype(F32)
    node_back[...] = (cot_sum * node_slope[...]).astype(BF)
    copies[4].wait()
    grad_agg[...] = dot_nt(node_back[...], w_node[WIDTH:, :]).astype(BF)
    copies[5].wait()
    grad_gathered[...] = dot_nt(grad_agg[...], w_msg[...]).astype(BF)
    direct[...] = cot_sum + dot_nt(node_back[...], w_node[:WIDTH, :]).astype(BF).astype(F32)

    for copy in copies[6:13]:
        copy.wait()
    flat[1024:1536, :] = dot_t(gathered[...], grad_agg[...])
    flat[1536:2048, :] = dot_t(latent[...], node_back[...])
    flat[2048:2560, :] = dot_t(aggregate[...], node_back[...])
    flat[2560:3072, :] = dot_t(mid[...], mid_back[...])
    flat[3072:, :] = dot_t(up_agg[...], mid_back[...])
    part_cores(flat, 5, 11, stage)
    rest = pl.ds(560, 1232)
    store(stage.at[mine, rest], keep_far.at[rest])
    store(stage.at[1 - mine, rest], send_far.at[rest])

    for copy in copies[13:]:
        copy.wait()
    lane = iota((128, 128), 1)
    for start in range(0, EDGES, STEP):
        for at in range(start, start + STEP, 128):
            target = across(piece(dst, at, 128))
            for j in range(0, NODES, 128):
                targets[at : at + 128, j : j + 128] = ones(target == lane + j)
        grad = dot(targets[start : start + STEP, :], grad_gathered[...])
        grad = (grad * edge_slope[start : start + STEP, :].astype(F32)).astype(BF)
        from_src = dot(down(live_row(piece(src, start, STEP), count[0], start), EXT), grad)
        from_dst = dot(down(live_row(piece(dst, start, STEP), count[0], start), NODES), grad)
        if start == 0:
            total[:EXT, :] = from_src
            total[EXT:, :] = from_dst
        else:
            total[:EXT, :] += from_src
            total[EXT:, :] += from_dst
    grad_ends[...] = total[...].astype(BF)
    rims[...] = dot_nt(grad_ends[NODES:EXT, :], w_src[...]).astype(BF)
    store(rims.at[pl.ds(0, RIM)], low_far)
    store(rims.at[pl.ds(RIM, RIM)], high_far)

    grad = dot_t(lower[...], grad_ends[NODES : NODES + RIM, :])
    grad = grad + dot_t(upper[...], grad_ends[NODES + RIM : EXT, :])
    flat[:512, :] = grad + dot_t(latent[...], grad_ends[:NODES, :])
    flat[512:1024, :] = dot_t(latent[...], grad_ends[EXT:, :])
    part_cores(flat, 0, 5, stage)
    head = pl.ds(0, 560)
    store(stage.at[mine, head], keep_far.at[head])
    store(stage.at[1 - mine, head], send_far.at[head])
    grad = dot_nt(grad_ends[:NODES, :], w_src[...]) + dot_nt(grad_ends[EXT:, :], w_dst[...])
    direct[...] += grad
    store(direct, direct_far)
    for copy in stores:
        copy.wait()


def sheet_body(keep, got, out, rows, held):
    for pair in range(2 * ZN):
        at = 112 * pair
        rows[pair] = keep[at : at + 112, :].astype(F32) + got[at : at + 112, :].astype(F32)
        for h in range(2):
            for x in range(XN):
                to = (2 * (pair % 2) + h) * XN + x
                start = 14 * (pair // 2)
                held[to, start : start + 14, :] = rows[pair, 56 * h + 14 * x : 56 * h + 14 * x + 14, :]
    for to in range(YN * XN):
        out[to] = held[to].astype(BF)


def pillar_body(got, out, rows):
    total = got[0].astype(F32)
    for i in range(1, YN * XN):
        total = total + got[i].astype(F32)
    rows[:112, :] = total
    rows[112:, :] = jnp.zeros((16, WIDTH), F32)
    for z in range(ZN):
        out[z] = rows[14 * z : 14 * z + 16, :].astype(BF)


def last_body(got, out):
    total = got[0].astype(F32)
    for z in range(1, ZN):
        total = total + got[z].astype(F32)
    for r in range(TALL):
        for j in range(WIDTH // 128):
            out[4 * r + j : 4 * r + j + 1, :] = total[r : r + 1, 128 * j : 128 * (j + 1)]


def final_body(direct, from_low, from_high, index_far, grad_fine, index, sems):
    (copy,) = fetch(sems, (index_far, index))
    copy.wait()
    row = jnp.concatenate([piece(index, 0, 128), piece(index, 128, 64)], axis=1)
    total = direct[...] + dot(down(row[:, :RIM], NODES), from_low[...])
    total = total + dot(down(row[:, RIM:], NODES), from_high[...])
    grad_fine[...] = total.astype(BF)


def on_device(
    fine_latent,
    mid_latent,
    send_index,
    edge_src,
    edge_dst,
    edge_count,
    up_row,
    up_node,
    w_src,
    w_dst,
    w_msg,
    w_node,
    w_mid,
    cot_fine,
    cot_mid,
):
    core = (lax.axis_index("row") % CN).astype(jnp.int32).reshape(1)
    dest = up_row.reshape(1, NODES)
    ahead = [(i, (i + 1) % 256) for i in range(256)]
    behind = [(j, i) for i, j in ahead]
    line = lambda n: pltpu.VMEM((n,), jnp.int32)
    hold = lambda *shape: pltpu.VMEM(shape, BF)
    wide = lambda *shape: pltpu.VMEM(shape, F32)
    rim, fine, mid = bf(RIM, WIDTH), bf(NODES, WIDTH), bf(MIDS, WIDTH)

    low, high = run(
        send_body,
        (rim, rim),
        (send_index, fine_latent),
        "hh>vv",
        (line(2 * RIM), hold(NODES, WIDTH)),
        copies=2,
        mib=60,
    )
    lower = lax.ppermute(high, BOTH, ahead)
    upper = lax.ppermute(low, BOTH, behind)
    near, mine, spot = run(
        local_body,
        (fine, fine, i32(1, NODES)),
        (dest, fine_latent, w_src, w_dst),
        "hhhh>vvv",
        (pltpu.VMEM((1, NODES), jnp.int32), hold(NODES, WIDTH), hold(WIDTH, WIDTH))
        + (hold(WIDTH, WIDTH),),
        copies=4,
        mib=60,
        flops=4 * NODES * WIDTH * WIDTH,
    )
    dma = pltpu.SemaphoreType.DMA
    fine_out, sent, node_slope, edge_slope, gathered, aggregate = run(
        forward_body,
        (fine, bf(PLANE, CARRY, WIDTH), f32(NODES, WIDTH), bf(EDGES, WIDTH), fine, fine),
        (edge_count, edge_src, edge_dst, near, mine, w_src, lower, upper, w_msg, w_node)
        + (fine_latent, spot, up_node),
        "s" + 12 * "h" + ">hhhhhh",
        (line(EDGES), line(EDGES), hold(NODES, WIDTH), hold(WIDTH, WIDTH), hold(RIM, WIDTH))
        + (hold(RIM, WIDTH), hold(WIDTH, WIDTH), hold(2 * WIDTH, WIDTH), hold(NODES, WIDTH))
        + (pltpu.VMEM((1, NODES), jnp.int32), line(NODES), hold(NODES, WIDTH))
        + (hold(PLANE, CARRY, WIDTH), wide(NODES, WIDTH), hold(EDGES, WIDTH))
        + (hold(NODES, WIDTH), hold(NODES, WIDTH), hold(ENDS, WIDTH), hold(EDGES, ENDS))
        + (dma((12,)), dma((9,))),
        mib=60,
        flops=4 * 10**9,
    )
    got = lax.all_to_all(sent, "row", 0, 0, axis_index_groups=PLANES)
    sums, owner = run(sum_body, (bf(ZN, MIDS, WIDTH), i32(PLANE, 128)), (got,), "v>vv")
    got = lax.all_to_all(sums, "row", 0, 0, axis_index_groups=PILLARS)
    mid_out, grad_mid, spread, up_agg, mid_back = run(
        mid_body,
        (mid, mid, bf(ZN, MIDS, WIDTH), mid, mid),
        (got, mid_latent, cot_mid, w_mid),
        "vhhh>vvvvv",
        (hold(MIDS, WIDTH), hold(MIDS, WIDTH), hold(2 * WIDTH, WIDTH)),
        copies=3,
    )
    got = lax.all_to_all(spread, "row", 0, 0, axis_index_groups=PILLARS)
    (back,) = run(spread_body, (bf(PLANE, SLOTS, WIDTH),), (owner, got), "vv>v")
    back = lax.all_to_all(back, "row", 0, 0, axis_index_groups=PLANES)
    direct, low, high, keep, send = run(
        backward_body,
        (f32(NODES, WIDTH), rim, rim, bf(1792, WIDTH), bf(1792, WIDTH)),
        (edge_count, core, spot, back, cot_fine, node_slope, w_node, w_msg, edge_dst, gathered)
        + (fine_latent, aggregate, mid_latent, mid_back, up_agg, edge_src, edge_slope, lower)
        + (upper, w_src, w_dst),
        "ss" + 19 * "h" + ">hhhhh",
        (pltpu.VMEM((1, NODES), jnp.int32), hold(PLANE, SLOTS, WIDTH), hold(NODES, WIDTH))
        + (wide(NODES, WIDTH), hold(2 * WIDTH, WIDTH), hold(WIDTH, WIDTH), line(EDGES))
        + (hold(NODES, WIDTH), hold(NODES, WIDTH), hold(NODES, WIDTH), hold(MIDS, WIDTH))
        + (hold(MIDS, WIDTH), hold(MIDS, WIDTH), line(EDGES), hold(EDGES, WIDTH))
        + (hold(RIM, WIDTH), hold(RIM, WIDTH), hold(WIDTH, WIDTH), hold(WIDTH, WIDTH))
        + (hold(NODES, WIDTH), hold(NODES, WIDTH), hold(NODES, WIDTH))
        + (hold(EXT + NODES, WIDTH), hold(2 * RIM, WIDTH), wide(NODES, WIDTH))
        + (hold(EDGES, NODES), wide(EXT + NODES, WIDTH), wide(3584, WIDTH))
        + (hold(CN, 1792, WIDTH), dma((19,)), dma((7,))),
        mib=60,
        flops=5 * 10**9,
    )
    from_low = lax.ppermute(high, BOTH, ahead)
    from_high = lax.ppermute(low, BOTH, behind)
    got = lax.ppermute(send, BOTH, shift(dc=1))
    (grad_fine,) = run(
        final_body,
        (fine,),
        (direct, from_low, from_high, send_index),
        "vvvh>v",
        (line(2 * RIM),),
        copies=1,
        flops=2 * 10**8,
    )
    sheet = YN * XN
    (part,) = run(
        sheet_body,
        (bf(sheet, 112, WIDTH),),
        (keep, got),
        "vv>v",
        (wide(2 * ZN, 112, WIDTH), wide(sheet, 112, WIDTH)),
        mib=24,
    )
    part = lax.all_to_all(part, BOTH, 0, 0, axis_index_groups=SHEETS)
    (part,) = run(
        pillar_body, (bf(ZN, HELD, WIDTH),), (part,), "v>v", (wide(128, WIDTH),)
    )
    part = lax.all_to_all(part, "row", 0, 0, axis_index_groups=PILLARS)
    (weight_grads,) = run(last_body, (f32(56, 128),), (part,), "v>v")
    return fine_out, mid_out, grad_fine, grad_mid, weight_grads.reshape(-1)


def solution(mesh):
    rows, line = P(BOTH, None), P(BOTH)
    return jax.shard_map(
        on_device,
        mesh=mesh,
        in_specs=(rows, rows, line, line, line, line, rows, line)
        + (P(),) * 5
        + (rows, rows),
        out_specs=(rows, rows, rows, rows, line),
        check_vma=False,
    )
```

```python
import jax
import jax.numpy as jnp
from jax import lax
from jax.experimental import pallas as pl
from jax.experimental.pallas import tpu as pltpu
from jax.sharding import PartitionSpec as P

BF = jnp.bfloat16
F32 = jnp.float32
BOTH = ("row", "col")
CAP = 12
ZN, YN, CN, XN = 8, 4, 2, 4
PLANE = YN * CN
NODES, RIM, EXT, MIDS, WIDTH, EDGES = 384, 96, 576, 32, 512, 2304
SLOTS = ZN * CAP
CARRY = 112
STEP = 768
DST = 640
ENDS = DST + NODES
TALL = 14
HELD = 16


def place(z, y, c, x):
    return ((z * YN + y) * CN + c) * XN + x


def shift(dz=0, dy=0, dc=0, dx=0):
    return [
        (place(z, y, c, x), place((z + dz) % ZN, (y + dy) % YN, (c + dc) % CN, (x + dx) % XN))
        for z in range(ZN)
        for y in range(YN)
        for c in range(CN)
        for x in range(XN)
    ]


PLANES = [[z * PLANE + i for i in range(PLANE)] for z in range(ZN)]
PILLARS = [[z * PLANE + i for z in range(ZN)] for i in range(PLANE)]
SHEETS = [
    [place(z, y, c, x) for y in range(YN) for x in range(XN)] for z in range(ZN) for c in range(CN)
]


PEERS = ((0, 0), (2, 0), (2, 1), (1, 0), (1, 1), (3, 0), (3, 1), (0, 1))


def peer(me, dy, dc):
    return (((me >> 1) + dy) & (YN - 1)) * CN + ((me & 1) ^ dc)


def dot(a, b):
    return jnp.dot(a, b, preferred_element_type=F32)


def dot_t(a, b):
    return lax.dot_general(a, b, (((0,), (0,)), ((), ())), preferred_element_type=F32)


def dot_nt(a, b):
    return lax.dot_general(a, b, (((1,), (1,)), ((), ())), preferred_element_type=F32)


def iota(shape, axis):
    return lax.broadcasted_iota(jnp.int32, shape, axis)


def ones(mask):
    return jnp.where(mask, 1.0, 0.0).astype(BF)


def across(row):
    return jnp.transpose(jnp.broadcast_to(row, (128, 128)))


def down(row, count, start=0):
    return ones(iota((count, row.shape[1]), 0) + start == row)


def silu_pair(u):
    s = 0.5 * jnp.tanh(0.5 * u) + 0.5
    return u * s, s * (1.0 + u * (1.0 - s))


def bf(*shape):
    return jax.ShapeDtypeStruct(shape, BF)


def f32(*shape):
    return jax.ShapeDtypeStruct(shape, F32)


def i32(*shape):
    return jax.ShapeDtypeStruct(shape, jnp.int32)


def run(body, outs, args, kinds, scratch=(), copies=0, mib=16, flops=0):
    spaces = {"s": pltpu.SMEM, "v": pltpu.VMEM, "h": pltpu.HBM}
    moved = sum(a.size * a.dtype.itemsize for a in list(args) + list(outs))
    took, gave = kinds.split(">")
    scratch = list(scratch)
    if copies:
        scratch.append(pltpu.SemaphoreType.DMA((copies,)))
    return pl.pallas_call(
        body,
        out_shape=list(outs),
        in_specs=[pl.BlockSpec(memory_space=spaces[k]) for k in took],
        out_specs=[pl.BlockSpec(memory_space=spaces[k]) for k in gave],
        scratch_shapes=scratch,
        compiler_params=pltpu.CompilerParams(vmem_limit_bytes=mib << 20),
        cost_estimate=pl.CostEstimate(flops=flops, bytes_accessed=moved, transcendentals=0),
    )(*args)


def fetch(sems, *pairs):
    copies = [pltpu.make_async_copy(a, b, sems.at[i]) for i, (a, b) in enumerate(pairs)]
    for copy in copies:
        copy.start()
    return copies


def piece(line, start, size):
    return line[pl.ds(start, size)].reshape(1, size)


def send_body(index_far, latent_far, low, high, index, latent, sems):
    for copy in fetch(sems, (index_far, index), (latent_far, latent)):
        copy.wait()
    row = jnp.concatenate([piece(index, 0, 128), piece(index, 128, 64)], axis=1)
    rows = dot_t(down(row, NODES), latent[...]).astype(BF)
    low[...] = rows[:RIM]
    high[...] = rows[RIM:]


def local_body(
    dest_far, latent_far, w_src_far, w_dst_far, near, mine, spot, dest, latent, w_src, w_dst, sems
):
    copies = fetch(
        sems, (dest_far, dest), (latent_far, latent), (w_src_far, w_src), (w_dst_far, w_dst)
    )
    copies[0].wait()
    for j in range(NODES // 128):
        row = dest[:, 128 * j : 128 * (j + 1)]
        rank = jnp.zeros((1, 128), F32)
        for b in range(j + 1):
            same = across(dest[:, 128 * b : 128 * (b + 1)]) == row
            if b == j:
                same = same & (iota((128, 128), 0) < iota((128, 128), 1))
            rank = rank + jnp.sum(jnp.where(same, 1.0, 0.0), axis=0, keepdims=True)
        spot[:, 128 * j : 128 * (j + 1)] = (
            (row & (PLANE - 1)) * SLOTS + (row >> 3) * CAP + rank.astype(jnp.int32)
        )
    for copy in copies[1:]:
        copy.wait()
    near[...] = dot(latent[...], w_src[...]).astype(BF)
    mine[...] = dot(latent[...], w_dst[...]).astype(BF)


def live_row(row, count, start):
    return jnp.where(iota(row.shape, 1) + start < count, row, -1)


def forward_body(
    count,
    place_at,
    src_far,
    dst_far,
    near_far,
    mine_far,
    w_src_far,
    lower_far,
    upper_far,
    w_msg_far,
    w_node_far,
    latent_far,
    spot_far,
    node_far,
    fine_out_far,
    node_slope_far,
    slope_far,
    gathered_far,
    aggregate_far,
    *rest,
):
    sent_far, rest = rest[:PLANE], rest[PLANE:]
    src, dst, mine, w_src, lower, upper, w_msg, w_node, latent, spot, node = rest[:11]
    fine_out, sent, node_slope, edge_slope, gathered, aggregate = rest[11:17]
    table, ends, sems, out_sems = rest[17:]
    near = table.at[:NODES, :]
    copies = fetch(
        sems,
        (src_far, src),
        (dst_far, dst),
        (w_src_far, w_src),
        (lower_far, lower),
        (upper_far, upper),
        (near_far, near),
        (mine_far, mine),
        (w_msg_far, w_msg),
        (w_node_far, w_node),
        (latent_far, latent),
        (spot_far, spot),
        (node_far, node),
    )
    stores = []

    def store(here, there):
        stores.append(pltpu.make_async_copy(here, there, out_sems.at[len(stores)]))
        stores[-1].start()

    table[EXT:DST, :] = jnp.zeros((DST - EXT, WIDTH), BF)
    for copy in copies[:2]:
        copy.wait()
    lane = iota((128, 128), 1)
    total = jnp.zeros((NODES, WIDTH), F32)
    for start in range(0, EDGES, STEP):
        for at in range(start, start + STEP, 128):
            source, target = across(piece(src, at, 128)), across(piece(dst, at, 128))
            for j in range(0, DST, 128):
                ends[at : at + 128, j : j + 128] = ones(source == lane + j)
            for j in range(0, NODES, 128):
                ends[at : at + 128, DST + j : DST + j + 128] = ones(target == lane + j)
        if start == 0:
            for copy in copies[2:7]:
                copy.wait()
            table[DST:, :] = mine[...]
            table[NODES : NODES + RIM, :] = dot(lower[...], w_src[...]).astype(BF)
            table[NODES + RIM : EXT, :] = dot(upper[...], w_src[...]).astype(BF)
        act, slope = silu_pair(dot(ends[start : start + STEP, :], table[...]))
        here = pl.ds(start, STEP)
        edge_slope[here, :] = slope.astype(BF)
        store(edge_slope.at[here, :], slope_far.at[here, :])
        row = live_row(piece(dst, start, STEP), count[0], start)
        total = total + dot(down(row, NODES), act.astype(BF))
    gathered[...] = total.astype(BF)
    store(gathered, gathered_far)
    for copy in copies[7:]:
        copy.wait()
    aggregate[...] = dot(gathered[...], w_msg[...]).astype(BF)
    store(aggregate, aggregate_far)
    update = dot(latent[...], w_node[:WIDTH, :]) + dot(aggregate[...], w_node[WIDTH:, :])
    lift, slope = silu_pair(update)
    node_slope[...] = slope
    store(node_slope, node_slope_far)
    fine_out[...] = (latent[...].astype(F32) + lift).astype(BF)
    store(fine_out, fine_out_far)
    names = jnp.broadcast_to((piece(node, 0, NODES) + 1).astype(F32), (16, NODES)).astype(BF)
    for i, (dy, dc) in enumerate(PEERS):
        offset = spot[...] - peer(place_at[0], dy, dc) * SLOTS
        to_slot = ones((iota((128, NODES), 0) == offset) & (offset < SLOTS))
        sent[i] = dot(to_slot[:CARRY], fine_out[...]).astype(BF)
        sent[i, SLOTS:CARRY, :128] = dot_nt(names, to_slot).astype(BF)
        store(sent.at[i], sent_far[i])
    for copy in stores:
        copy.wait()


def sum_body(*refs):
    got, (sums, owner) = refs[:PLANE], refs[PLANE:]
    total = jnp.zeros((ZN * MIDS, WIDTH), F32)
    level = iota((1, 128), 1)
    base = jnp.zeros((1, 128), jnp.int32)
    for z in range(1, ZN):
        base = base + jnp.where(level >= z * CAP, MIDS, 0)
    for i in range(PLANE):
        name = got[i][SLOTS:CARRY, :128][:1].astype(F32).astype(jnp.int32)
        name = jnp.where((name > 0) & (level < SLOTS), name - 1 + base, -1)
        owner[i : i + 1, :] = name
        total = total + dot(down(name, ZN * MIDS)[:, :CARRY], got[i][...])
    for z in range(ZN):
        sums[z] = total[z * MIDS : (z + 1) * MIDS].astype(BF)


def mid_body(
    got,
    latent_far,
    cot_far,
    w_mid_far,
    spread,
    mid_out_far,
    grad_mid_far,
    up_agg_far,
    mid_back_far,
    latent,
    cot,
    w_mid,
    mid_out,
    grad_mid,
    up_agg,
    mid_back,
    sems,
):
    copies = fetch(sems, (latent_far, latent), (cot_far, cot), (w_mid_far, w_mid))
    total = got[0].astype(F32)
    for z in range(1, ZN):
        total = total + got[z].astype(F32)
    agg = (0.25 * total).astype(BF)
    up_agg[...] = agg
    for copy in copies:
        copy.wait()
    update = dot(latent[...], w_mid[:WIDTH, :]) + dot(agg, w_mid[WIDTH:, :])
    lift, slope = silu_pair(update)
    mid_out[...] = (latent[...].astype(F32) + lift).astype(BF)
    back = (cot[...].astype(F32) * slope).astype(BF)
    mid_back[...] = back
    stores = [
        pltpu.make_async_copy(up_agg, up_agg_far, sems.at[3]),
        pltpu.make_async_copy(mid_out, mid_out_far, sems.at[4]),
        pltpu.make_async_copy(mid_back, mid_back_far, sems.at[5]),
        pltpu.make_async_copy(grad_mid, grad_mid_far, sems.at[6]),
    ]
    for copy in stores[:3]:
        copy.start()
    grad = dot_nt(back, w_mid[:WIDTH, :]).astype(BF).astype(F32)
    grad_mid[...] = (cot[...].astype(F32) + grad).astype(BF)
    stores[3].start()
    grad = dot_nt(back, w_mid[WIDTH:, :]).astype(BF).astype(F32)
    grad = (0.25 * grad).astype(BF)
    for z in range(ZN):
        spread[z] = grad
    for copy in stores:
        copy.wait()


def spread_body(owner, got, *back):
    rows = jnp.concatenate([got[z] for z in range(ZN)], axis=0)
    for i in range(PLANE):
        back[i][...] = dot_t(down(owner[i : i + 1, :], ZN * MIDS), rows)[:SLOTS].astype(BF)


def part_cores(flat, first, pairs, stage):
    for pair in range(first, first + pairs):
        for c in range(CN):
            rows = [flat[pl.ds(224 * pair + 112 * h + 56 * c, 56), :] for h in range(2)]
            rows = jnp.concatenate(rows, axis=0).astype(BF)
            stage[c, 112 * pair : 112 * (pair + 1), :] = rows


def backward_body(
    count,
    place_at,
    *refs,
):
    (
    spot_far,
    cot_far,
    node_slope_far,
    w_node_far,
    w_msg_far,
    dst_far,
    gathered_far,
    latent_far,
    aggregate_far,
    mid_far,
    mid_back_far,
    up_agg_far,
    src_far,
    slope_far,
    lower_far,
    upper_far,
    w_src_far,
    w_dst_far,
    ) = refs[:18]
    back_far, refs = refs[18 : 18 + PLANE], refs[18 + PLANE :]
    direct_far, low_far, high_far, keep_far, send_far = refs[:5]
    spot, back, cot, node_slope, w_node, w_msg, dst, gathered, latent, aggregate = refs[5:15]
    mid, mid_back, up_agg, src, edge_slope, lower, upper, w_src, w_dst = refs[15:24]
    node_back, grad_agg, grad_gathered, grad_ends, rims, direct = refs[24:30]
    targets, total, flat, stage, sems, out_sems = refs[30:]
    copies = fetch(
        sems,
        (spot_far, spot),
        *[(back_far[i], back.at[i]) for i in range(PLANE)],
        (cot_far, cot),
        (node_slope_far, node_slope),
        (w_node_far, w_node),
        (w_msg_far, w_msg),
        (dst_far, dst),
        (gathered_far, gathered),
        (latent_far, latent),
        (aggregate_far, aggregate),
        (mid_far, mid),
        (mid_back_far, mid_back),
        (up_agg_far, up_agg),
        (src_far, src),
        (slope_far, edge_slope),
        (lower_far, lower),
        (upper_far, upper),
        (w_src_far, w_src),
        (w_dst_far, w_dst),
    )
    stores = []

    def store(here, there):
        stores.append(pltpu.make_async_copy(here, there, out_sems.at[len(stores)]))
        stores[-1].start()

    mine = place_at[0] & 1
    for copy in copies[:9]:
        copy.wait()
    copies = copies[7:]
    up = jnp.zeros((NODES, WIDTH), F32)
    for i, (dy, dc) in enumerate(PEERS):
        offset = spot[...] - peer(place_at[0], dy, dc) * SLOTS
        up = up + dot_t(down(offset, SLOTS), back[i])
    for copy in copies[2:4]:
        copy.wait()
    cot_sum = (cot[...].astype(F32) + up).astype(BF).astype(F32)
    node_back[...] = (cot_sum * node_slope[...]).astype(BF)
    copies[4].wait()
    grad_agg[...] = dot_nt(node_back[...], w_node[WIDTH:, :]).astype(BF)
    copies[5].wait()
    grad_gathered[...] = dot_nt(grad_agg[...], w_msg[...]).astype(BF)
    direct[...] = cot_sum + dot_nt(node_back[...], w_node[:WIDTH, :]).astype(BF).astype(F32)

    for copy in copies[6:13]:
        copy.wait()
    flat[1024:1536, :] = dot_t(gathered[...], grad_agg[...])
    flat[1536:2048, :] = dot_t(latent[...], node_back[...])
    flat[2048:2560, :] = dot_t(aggregate[...], node_back[...])
    flat[2560:3072, :] = dot_t(mid[...], mid_back[...])
    flat[3072:, :] = dot_t(up_agg[...], mid_back[...])
    part_cores(flat, 5, 11, stage)
    rest = pl.ds(560, 1232)
    store(stage.at[mine, rest], keep_far.at[rest])
    store(stage.at[1 - mine, rest], send_far.at[rest])

    for copy in copies[13:]:
        copy.wait()
    lane = iota((128, 128), 1)
    for start in range(0, EDGES, STEP):
        for at in range(start, start + STEP, 128):
            target = across(piece(dst, at, 128))
            for j in range(0, NODES, 128):
                targets[at : at + 128, j : j + 128] = ones(target == lane + j)
        grad = dot(targets[start : start + STEP, :], grad_gathered[...])
        grad = (grad * edge_slope[start : start + STEP, :].astype(F32)).astype(BF)
        from_src = dot(down(live_row(piece(src, start, STEP), count[0], start), EXT), grad)
        from_dst = dot(down(live_row(piece(dst, start, STEP), count[0], start), NODES), grad)
        if start == 0:
            total[:EXT, :] = from_src
            total[EXT:, :] = from_dst
        else:
            total[:EXT, :] += from_src
            total[EXT:, :] += from_dst
    grad_ends[...] = total[...].astype(BF)
    rims[...] = dot_nt(grad_ends[NODES:EXT, :], w_src[...]).astype(BF)
    store(rims.at[pl.ds(0, RIM)], low_far)
    store(rims.at[pl.ds(RIM, RIM)], high_far)

    grad = dot_t(lower[...], grad_ends[NODES : NODES + RIM, :])
    grad = grad + dot_t(upper[...], grad_ends[NODES + RIM : EXT, :])
    flat[:512, :] = grad + dot_t(latent[...], grad_ends[:NODES, :])
    flat[512:1024, :] = dot_t(latent[...], grad_ends[EXT:, :])
    part_cores(flat, 0, 5, stage)
    head = pl.ds(0, 560)
    store(stage.at[mine, head], keep_far.at[head])
    store(stage.at[1 - mine, head], send_far.at[head])
    grad = dot_nt(grad_ends[:NODES, :], w_src[...]) + dot_nt(grad_ends[EXT:, :], w_dst[...])
    direct[...] += grad
    store(direct, direct_far)
    for copy in stores:
        copy.wait()


def sheet_body(keep, got, out, rows, held):
    for pair in range(2 * ZN):
        at = 112 * pair
        rows[pair] = keep[at : at + 112, :].astype(F32) + got[at : at + 112, :].astype(F32)
        for h in range(2):
            for x in range(XN):
                to = (2 * (pair % 2) + h) * XN + x
                start = 14 * (pair // 2)
                held[to, start : start + 14, :] = rows[pair, 56 * h + 14 * x : 56 * h + 14 * x + 14, :]
    for to in range(YN * XN):
        out[to] = held[to].astype(BF)


def pillar_body(
    got,
    low_far,
    high_far,
    direct_far,
    index_far,
    out,
    grad_fine_far,
    low,
    high,
    direct,
    index,
    grad_fine,
    rows,
    sems,
):
    copies = fetch(
        sems, (index_far, index), (low_far, low), (high_far, high), (direct_far, direct)
    )
    total = got[0].astype(F32)
    for i in range(1, YN * XN):
        total = total + got[i].astype(F32)
    rows[:112, :] = total
    rows[112:, :] = jnp.zeros((16, WIDTH), F32)
    for z in range(ZN):
        out[z] = rows[14 * z : 14 * z + 16, :].astype(BF)
    for copy in copies:
        copy.wait()
    row = jnp.concatenate([piece(index, 0, 128), piece(index, 128, 64)], axis=1)
    total = direct[...] + dot(down(row[:, :RIM], NODES), low[...])
    total = total + dot(down(row[:, RIM:], NODES), high[...])
    grad_fine[...] = total.astype(BF)
    copy = pltpu.make_async_copy(grad_fine, grad_fine_far, sems.at[4])
    copy.start()
    copy.wait()


def last_body(got, out):
    total = got[0].astype(F32)
    for z in range(1, ZN):
        total = total + got[z].astype(F32)
    for r in range(TALL):
        for j in range(WIDTH // 128):
            here = pl.ds(WIDTH * r + 128 * j, 128)
            out[here] = total[r : r + 1, 128 * j : 128 * (j + 1)].reshape(128)


def on_device(
    fine_latent,
    mid_latent,
    send_index,
    edge_src,
    edge_dst,
    edge_count,
    up_row,
    up_node,
    w_src,
    w_dst,
    w_msg,
    w_node,
    w_mid,
    cot_fine,
    cot_mid,
):
    place_at = (lax.axis_index("row") % PLANE).astype(jnp.int32).reshape(1)
    dest = up_row.reshape(1, NODES)
    ahead = [(i, (i + 1) % 256) for i in range(256)]
    behind = [(j, i) for i, j in ahead]
    line = lambda n: pltpu.VMEM((n,), jnp.int32)
    hold = lambda *shape: pltpu.VMEM(shape, BF)
    wide = lambda *shape: pltpu.VMEM(shape, F32)
    rim, fine, mid = bf(RIM, WIDTH), bf(NODES, WIDTH), bf(MIDS, WIDTH)

    low, high = run(
        send_body,
        (rim, rim),
        (send_index, fine_latent),
        "hh>vv",
        (line(2 * RIM), hold(NODES, WIDTH)),
        copies=2,
        mib=60,
    )
    lower = lax.ppermute(high, BOTH, ahead)
    upper = lax.ppermute(low, BOTH, behind)
    near, mine, spot = run(
        local_body,
        (fine, fine, i32(1, NODES)),
        (dest, fine_latent, w_src, w_dst),
        "hhhh>vvv",
        (pltpu.VMEM((1, NODES), jnp.int32), hold(NODES, WIDTH), hold(WIDTH, WIDTH))
        + (hold(WIDTH, WIDTH),),
        copies=4,
        mib=60,
        flops=4 * NODES * WIDTH * WIDTH,
    )
    dma = pltpu.SemaphoreType.DMA
    fine_out, node_slope, edge_slope, gathered, aggregate, *sent = run(
        forward_body,
        (fine, f32(NODES, WIDTH), bf(EDGES, WIDTH), fine, fine) + PLANE * (bf(CARRY, WIDTH),),
        (edge_count, place_at, edge_src, edge_dst, near, mine, w_src, lower, upper, w_msg, w_node)
        + (fine_latent, spot, up_node),
        "ss" + 12 * "h" + ">" + 13 * "h",
        (line(EDGES), line(EDGES), hold(NODES, WIDTH), hold(WIDTH, WIDTH), hold(RIM, WIDTH))
        + (hold(RIM, WIDTH), hold(WIDTH, WIDTH), hold(2 * WIDTH, WIDTH), hold(NODES, WIDTH))
        + (pltpu.VMEM((1, NODES), jnp.int32), line(NODES), hold(NODES, WIDTH))
        + (hold(PLANE, CARRY, WIDTH), wide(NODES, WIDTH), hold(EDGES, WIDTH))
        + (hold(NODES, WIDTH), hold(NODES, WIDTH), hold(ENDS, WIDTH), hold(EDGES, ENDS))
        + (dma((12,)), dma((15,))),
        mib=60,
        flops=4 * 10**9,
    )
    got = [sent[0]]
    for (dy, dc), block in zip(PEERS[1:], sent[1:]):
        got.append(lax.ppermute(block, BOTH, shift(dy=dy, dc=dc)))
    sums, owner = run(sum_body, (bf(ZN, MIDS, WIDTH), i32(PLANE, 128)), got, 8 * "v" + ">vv")
    got = lax.all_to_all(sums, "row", 0, 0, axis_index_groups=PILLARS)
    spread, mid_out, grad_mid, up_agg, mid_back = run(
        mid_body,
        (bf(ZN, MIDS, WIDTH), mid, mid, mid, mid),
        (got, mid_latent, cot_mid, w_mid),
        "vhhh>vhhhh",
        (hold(MIDS, WIDTH), hold(MIDS, WIDTH), hold(2 * WIDTH, WIDTH))
        + 4 * (hold(MIDS, WIDTH),),
        copies=7,
    )
    got = lax.all_to_all(spread, "row", 0, 0, axis_index_groups=PILLARS)
    blocks = run(spread_body, PLANE * (bf(SLOTS, WIDTH),), (owner, got), "vv>" + 8 * "v")
    back = [blocks[0]]
    for (dy, dc), block in zip(PEERS[1:], blocks[1:]):
        back.append(lax.ppermute(block, BOTH, shift(dy=-dy, dc=-dc)))
    direct, low, high, keep, send = run(
        backward_body,
        (f32(NODES, WIDTH), rim, rim, bf(1792, WIDTH), bf(1792, WIDTH)),
        (edge_count, place_at, spot, cot_fine, node_slope, w_node, w_msg, edge_dst, gathered)
        + (fine_latent, aggregate, mid_latent, mid_back, up_agg, edge_src, edge_slope, lower)
        + (upper, w_src, w_dst, *back),
        "ss" + 26 * "h" + ">hhhhh",
        (pltpu.VMEM((1, NODES), jnp.int32), hold(PLANE, SLOTS, WIDTH), hold(NODES, WIDTH))
        + (wide(NODES, WIDTH), hold(2 * WIDTH, WIDTH), hold(WIDTH, WIDTH), line(EDGES))
        + (hold(NODES, WIDTH), hold(NODES, WIDTH), hold(NODES, WIDTH), hold(MIDS, WIDTH))
        + (hold(MIDS, WIDTH), hold(MIDS, WIDTH), line(EDGES), hold(EDGES, WIDTH))
        + (hold(RIM, WIDTH), hold(RIM, WIDTH), hold(WIDTH, WIDTH), hold(WIDTH, WIDTH))
        + (hold(NODES, WIDTH), hold(NODES, WIDTH), hold(NODES, WIDTH))
        + (hold(EXT + NODES, WIDTH), hold(2 * RIM, WIDTH), wide(NODES, WIDTH))
        + (hold(EDGES, NODES), wide(EXT + NODES, WIDTH), wide(3584, WIDTH))
        + (hold(CN, 1792, WIDTH), dma((26,)), dma((7,))),
        mib=60,
        flops=5 * 10**9,
    )
    from_low = lax.ppermute(high, BOTH, ahead)
    from_high = lax.ppermute(low, BOTH, behind)
    got = lax.ppermute(send, BOTH, shift(dc=1))
    sheet = YN * XN
    (part,) = run(
        sheet_body,
        (bf(sheet, 112, WIDTH),),
        (keep, got),
        "vv>v",
        (wide(2 * ZN, 112, WIDTH), wide(sheet, 112, WIDTH)),
        mib=24,
    )
    part, from_low, from_high = lax.optimization_barrier((part, from_low, from_high))
    part = lax.all_to_all(part, BOTH, 0, 0, axis_index_groups=SHEETS)
    part, grad_fine = run(
        pillar_body,
        (bf(ZN, HELD, WIDTH), fine),
        (part, from_low, from_high, direct, send_index),
        "vhhhh>vh",
        (hold(RIM, WIDTH), hold(RIM, WIDTH), wide(NODES, WIDTH), line(2 * RIM))
        + (hold(NODES, WIDTH), wide(128, WIDTH)),
        copies=5,
        mib=24,
    )
    part = lax.all_to_all(part, "row", 0, 0, axis_index_groups=PILLARS)
    (weight_grads,) = run(last_body, (f32(TALL * WIDTH),), (part,), "v>v")
    return fine_out, mid_out, grad_fine, grad_mid, weight_grads


def solution(mesh):
    rows, line = P(BOTH, None), P(BOTH)
    return jax.shard_map(
        on_device,
        mesh=mesh,
        in_specs=(rows, rows, line, line, line, line, rows, line)
        + (P(),) * 5
        + (rows, rows),
        out_specs=(rows, rows, rows, rows, line),
        check_vma=False,
    )
```

```python
import jax
import jax.numpy as jnp
from jax import lax
from jax.experimental import pallas as pl
from jax.experimental.pallas import tpu as pltpu
from jax.sharding import PartitionSpec as P

BF = jnp.bfloat16
F32 = jnp.float32
BOTH = ("row", "col")
CAP = 12
ZN, YN, CN, XN = 8, 4, 2, 4
PLANE = YN * CN
NODES, RIM, EXT, MIDS, WIDTH, EDGES = 384, 96, 576, 32, 512, 2304
SLOTS = ZN * CAP
CARRY = 112
STEP = 768
DST = 640
ENDS = DST + NODES
TALL = 14
HELD = 16
VMEM = 57_000_000


def place(z, y, c, x):
    return ((z * YN + y) * CN + c) * XN + x


def shift(dz=0, dy=0, dc=0, dx=0):
    return [
        (place(z, y, c, x), place((z + dz) % ZN, (y + dy) % YN, (c + dc) % CN, (x + dx) % XN))
        for z in range(ZN)
        for y in range(YN)
        for c in range(CN)
        for x in range(XN)
    ]


PLANES = [[z * PLANE + i for i in range(PLANE)] for z in range(ZN)]
PILLARS = [[z * PLANE + i for z in range(ZN)] for i in range(PLANE)]
SHEETS = [
    [place(z, y, c, x) for y in range(YN) for x in range(XN)] for z in range(ZN) for c in range(CN)
]


PEERS = ((0, 0), (2, 0), (2, 1), (1, 0), (1, 1), (3, 0), (3, 1), (0, 1))


def peer(me, dy, dc):
    return (((me >> 1) + dy) & (YN - 1)) * CN + ((me & 1) ^ dc)


def dot(a, b):
    return jnp.dot(a, b, preferred_element_type=F32)


def dot_t(a, b):
    return lax.dot_general(a, b, (((0,), (0,)), ((), ())), preferred_element_type=F32)


def dot_nt(a, b):
    return lax.dot_general(a, b, (((1,), (1,)), ((), ())), preferred_element_type=F32)


def iota(shape, axis):
    return lax.broadcasted_iota(jnp.int32, shape, axis)


def ones(mask):
    return jnp.where(mask, 1.0, 0.0).astype(BF)


def across(row):
    return jnp.transpose(jnp.broadcast_to(row, (128, 128)))


def down(row, count, start=0):
    return ones(iota((count, row.shape[1]), 0) + start == row)


def silu_pair(u):
    s = 0.5 * jnp.tanh(0.5 * u) + 0.5
    return u * s, s * (1.0 + u * (1.0 - s))


def bf(*shape):
    return jax.ShapeDtypeStruct(shape, BF)


def f32(*shape):
    return jax.ShapeDtypeStruct(shape, F32)


def i32(*shape):
    return jax.ShapeDtypeStruct(shape, jnp.int32)


def run(body, outs, args, kinds, scratch=(), copies=0, mib=16, room=0, flops=0):
    spaces = {"s": pltpu.SMEM, "v": pltpu.VMEM, "h": pltpu.HBM}
    moved = sum(a.size * a.dtype.itemsize for a in list(args) + list(outs))
    took, gave = kinds.split(">")
    scratch = list(scratch)
    limit = VMEM - room if room else mib << 20
    if copies:
        scratch.append(pltpu.SemaphoreType.DMA((copies,)))
    return pl.pallas_call(
        body,
        out_shape=list(outs),
        in_specs=[pl.BlockSpec(memory_space=spaces[k]) for k in took],
        out_specs=[pl.BlockSpec(memory_space=spaces[k]) for k in gave],
        scratch_shapes=scratch,
        compiler_params=pltpu.CompilerParams(vmem_limit_bytes=limit),
        cost_estimate=pl.CostEstimate(flops=flops, bytes_accessed=moved, transcendentals=0),
    )(*args)


def fetch(sems, *pairs):
    copies = [pltpu.make_async_copy(a, b, sems.at[i]) for i, (a, b) in enumerate(pairs)]
    for copy in copies:
        copy.start()
    return copies


def piece(line, start, size):
    return line[pl.ds(start, size)].reshape(1, size)


def send_body(index_far, latent_far, low, high, index, latent, sems):
    for copy in fetch(sems, (index_far, index), (latent_far, latent)):
        copy.wait()
    row = jnp.concatenate([piece(index, 0, 128), piece(index, 128, 64)], axis=1)
    rows = dot_t(down(row, NODES), latent[...]).astype(BF)
    low[...] = rows[:RIM]
    high[...] = rows[RIM:]


def local_body(
    dest_far, latent_far, w_src_far, w_dst_far, near, mine, spot, dest, latent, w_src, w_dst, sems
):
    copies = fetch(
        sems, (dest_far, dest), (latent_far, latent), (w_src_far, w_src), (w_dst_far, w_dst)
    )
    copies[0].wait()
    for j in range(NODES // 128):
        row = dest[:, 128 * j : 128 * (j + 1)]
        rank = jnp.zeros((1, 128), F32)
        for b in range(j + 1):
            same = across(dest[:, 128 * b : 128 * (b + 1)]) == row
            if b == j:
                same = same & (iota((128, 128), 0) < iota((128, 128), 1))
            rank = rank + jnp.sum(jnp.where(same, 1.0, 0.0), axis=0, keepdims=True)
        spot[:, 128 * j : 128 * (j + 1)] = (
            (row & (PLANE - 1)) * SLOTS + (row >> 3) * CAP + rank.astype(jnp.int32)
        )
    for copy in copies[1:]:
        copy.wait()
    near[...] = dot(latent[...], w_src[...]).astype(BF)
    mine[...] = dot(latent[...], w_dst[...]).astype(BF)


def live_row(row, count, start):
    return jnp.where(iota(row.shape, 1) + start < count, row, -1)


def forward_body(
    count,
    place_at,
    src_far,
    dst_far,
    near_far,
    mine_far,
    w_src_far,
    lower_far,
    upper_far,
    w_msg_far,
    w_node_far,
    latent_far,
    spot_far,
    node_far,
    fine_out_far,
    node_slope_far,
    slope_far,
    gathered_far,
    aggregate_far,
    rims_far,
    *rest,
):
    sent_far, rest = rest[:PLANE], rest[PLANE:]
    src, dst, mine, w_src, lower, upper, w_msg, w_node, latent, spot, node = rest[:11]
    fine_out, sent, node_slope, edge_slope, gathered, aggregate = rest[11:17]
    table, ends, sems, out_sems = rest[17:]
    near = table.at[:NODES, :]
    copies = fetch(
        sems,
        (src_far, src),
        (dst_far, dst),
        (w_src_far, w_src),
        (lower_far, lower),
        (upper_far, upper),
        (near_far, near),
        (mine_far, mine),
        (w_msg_far, w_msg),
        (w_node_far, w_node),
        (latent_far, latent),
        (spot_far, spot),
        (node_far, node),
    )
    stores = []

    def store(here, there):
        stores.append(pltpu.make_async_copy(here, there, out_sems.at[len(stores)]))
        stores[-1].start()

    table[EXT:DST, :] = jnp.zeros((DST - EXT, WIDTH), BF)
    for copy in copies[:2]:
        copy.wait()
    lane = iota((128, 128), 1)
    total = jnp.zeros((NODES, WIDTH), F32)
    for start in range(0, EDGES, STEP):
        for at in range(start, start + STEP, 128):
            source, target = across(piece(src, at, 128)), across(piece(dst, at, 128))
            for j in range(0, DST, 128):
                ends[at : at + 128, j : j + 128] = ones(source == lane + j)
            for j in range(0, NODES, 128):
                ends[at : at + 128, DST + j : DST + j + 128] = ones(target == lane + j)
        if start == 0:
            for copy in copies[2:7]:
                copy.wait()
            store(lower, rims_far.at[pl.ds(0, RIM)])
            store(upper, rims_far.at[pl.ds(RIM, RIM)])
            table[DST:, :] = mine[...]
            table[NODES : NODES + RIM, :] = dot(lower[...], w_src[...]).astype(BF)
            table[NODES + RIM : EXT, :] = dot(upper[...], w_src[...]).astype(BF)
        act, slope = silu_pair(dot(ends[start : start + STEP, :], table[...]))
        here = pl.ds(start, STEP)
        edge_slope[here, :] = slope.astype(BF)
        store(edge_slope.at[here, :], slope_far.at[here, :])
        row = live_row(piece(dst, start, STEP), count[0], start)
        total = total + dot(down(row, NODES), act.astype(BF))
    gathered[...] = total.astype(BF)
    store(gathered, gathered_far)
    for copy in copies[7:]:
        copy.wait()
    aggregate[...] = dot(gathered[...], w_msg[...]).astype(BF)
    store(aggregate, aggregate_far)
    update = dot(latent[...], w_node[:WIDTH, :]) + dot(aggregate[...], w_node[WIDTH:, :])
    lift, slope = silu_pair(update)
    node_slope[...] = slope
    store(node_slope, node_slope_far)
    fine_out[...] = (latent[...].astype(F32) + lift).astype(BF)
    store(fine_out, fine_out_far)
    names = jnp.broadcast_to((piece(node, 0, NODES) + 1).astype(F32), (16, NODES)).astype(BF)
    for i, (dy, dc) in enumerate(PEERS):
        offset = spot[...] - peer(place_at[0], dy, dc) * SLOTS
        to_slot = ones((iota((128, NODES), 0) == offset) & (offset < SLOTS))
        sent[i] = dot(to_slot[:CARRY], fine_out[...]).astype(BF)
        sent[i, SLOTS:CARRY, :128] = dot_nt(names, to_slot).astype(BF)
        store(sent.at[i], sent_far[i])
    for copy in stores:
        copy.wait()


def sum_body(*refs):
    got, (sums, owner) = refs[:PLANE], refs[PLANE:]
    total = jnp.zeros((ZN * MIDS, WIDTH), F32)
    level = iota((1, 128), 1)
    base = jnp.zeros((1, 128), jnp.int32)
    for z in range(1, ZN):
        base = base + jnp.where(level >= z * CAP, MIDS, 0)
    for i in range(PLANE):
        name = got[i][SLOTS:CARRY, :128][:1].astype(F32).astype(jnp.int32)
        name = jnp.where((name > 0) & (level < SLOTS), name - 1 + base, -1)
        owner[i : i + 1, :] = name
        total = total + dot(down(name, ZN * MIDS)[:, :CARRY], got[i][...])
    for z in range(ZN):
        sums[z] = total[z * MIDS : (z + 1) * MIDS].astype(BF)


def mid_body(
    got,
    latent_far,
    cot_far,
    w_mid_far,
    spread,
    up_agg,
    mid_back,
    mid_out_far,
    grad_mid_far,
    latent,
    cot,
    w_mid,
    mid_out,
    grad_mid,
    sems,
):
    copies = fetch(sems, (latent_far, latent), (cot_far, cot), (w_mid_far, w_mid))
    total = got[0].astype(F32)
    for z in range(1, ZN):
        total = total + got[z].astype(F32)
    agg = (0.25 * total).astype(BF)
    up_agg[...] = agg
    for copy in copies:
        copy.wait()
    update = dot(latent[...], w_mid[:WIDTH, :]) + dot(agg, w_mid[WIDTH:, :])
    lift, slope = silu_pair(update)
    mid_out[...] = (latent[...].astype(F32) + lift).astype(BF)
    back = (cot[...].astype(F32) * slope).astype(BF)
    mid_back[...] = back
    stores = [
        pltpu.make_async_copy(mid_out, mid_out_far, sems.at[3]),
        pltpu.make_async_copy(grad_mid, grad_mid_far, sems.at[4]),
    ]
    stores[0].start()
    grad = dot_nt(back, w_mid[:WIDTH, :]).astype(BF).astype(F32)
    grad_mid[...] = (cot[...].astype(F32) + grad).astype(BF)
    stores[1].start()
    grad = dot_nt(back, w_mid[WIDTH:, :]).astype(BF).astype(F32)
    grad = (0.25 * grad).astype(BF)
    for z in range(ZN):
        spread[z] = grad
    for copy in stores:
        copy.wait()


def spread_body(owner, got, *back):
    rows = jnp.concatenate([got[z] for z in range(ZN)], axis=0)
    for i in range(PLANE):
        back[i][...] = dot_t(down(owner[i : i + 1, :], ZN * MIDS), rows)[:SLOTS].astype(BF)


def part_cores(mine, flat, first, pairs, keep, send):
    for pair in range(first, first + pairs):
        even, odd = [
            jnp.concatenate(
                [flat[pl.ds(224 * pair + 112 * h + 56 * c, 56), :] for h in range(2)], axis=0
            )
            for c in range(CN)
        ]
        keep[112 * pair : 112 * (pair + 1), :] = jnp.where(mine == 0, even, odd).astype(BF)
        send[112 * pair : 112 * (pair + 1), :] = jnp.where(mine == 0, odd, even).astype(BF)


def backward_body(
    count,
    place_at,
    *refs,
):
    spot, up_agg, mid_back, cot, node_slope, w_node, w_msg, dst, gathered, latent = refs[:10]
    aggregate, mid, src, edge_slope, rims_in, w_src, w_dst = refs[10:17]
    back, refs = refs[17 : 17 + PLANE], refs[17 + PLANE :]
    direct, low, high, keep, send = refs[:5]
    node_back, grad_agg, grad_gathered, grad_ends, targets, total, flat = refs[5:]
    mine = place_at[0] & 1
    up = jnp.zeros((NODES, WIDTH), F32)
    for i, (dy, dc) in enumerate(PEERS):
        offset = spot[...] - peer(place_at[0], dy, dc) * SLOTS
        up = up + dot_t(down(offset, SLOTS), back[i][...])
    cot_sum = (cot[...].astype(F32) + up).astype(BF).astype(F32)
    node_back[...] = (cot_sum * node_slope[...]).astype(BF)
    grad_agg[...] = dot_nt(node_back[...], w_node[WIDTH:, :]).astype(BF)
    grad_gathered[...] = dot_nt(grad_agg[...], w_msg[...]).astype(BF)
    direct[...] = cot_sum + dot_nt(node_back[...], w_node[:WIDTH, :]).astype(BF).astype(F32)

    flat[1024:1536, :] = dot_t(gathered[...], grad_agg[...])
    flat[1536:2048, :] = dot_t(latent[...], node_back[...])
    flat[2048:2560, :] = dot_t(aggregate[...], node_back[...])
    flat[2560:3072, :] = dot_t(mid[...], mid_back[...])
    flat[3072:, :] = dot_t(up_agg[...], mid_back[...])
    part_cores(mine, flat, 5, 11, keep, send)

    lane = iota((128, 128), 1)
    for start in range(0, EDGES, STEP):
        for at in range(start, start + STEP, 128):
            target = across(piece(dst, at, 128))
            for j in range(0, NODES, 128):
                targets[at : at + 128, j : j + 128] = ones(target == lane + j)
        grad = dot(targets[start : start + STEP, :], grad_gathered[...])
        grad = (grad * edge_slope[start : start + STEP, :].astype(F32)).astype(BF)
        from_src = dot(down(live_row(piece(src, start, STEP), count[0], start), EXT), grad)
        from_dst = dot(down(live_row(piece(dst, start, STEP), count[0], start), NODES), grad)
        if start == 0:
            total[:EXT, :] = from_src
            total[EXT:, :] = from_dst
        else:
            total[:EXT, :] += from_src
            total[EXT:, :] += from_dst
    grad_ends[...] = total[...].astype(BF)
    rims = dot_nt(grad_ends[NODES:EXT, :], w_src[...]).astype(BF)
    low[...] = rims[:RIM]
    high[...] = rims[RIM:]
    grad = dot_t(rims_in[...], grad_ends[NODES:EXT, :])
    flat[:512, :] = grad + dot_t(latent[...], grad_ends[:NODES, :])
    flat[512:1024, :] = dot_t(latent[...], grad_ends[EXT:, :])
    part_cores(mine, flat, 0, 5, keep, send)
    grad = dot_nt(grad_ends[:NODES, :], w_src[...]) + dot_nt(grad_ends[EXT:, :], w_dst[...])
    direct[...] += grad


def sheet_body(keep, got, out, rows, held):
    for pair in range(2 * ZN):
        at = 112 * pair
        rows[pair] = keep[at : at + 112, :].astype(F32) + got[at : at + 112, :].astype(F32)
        for h in range(2):
            for x in range(XN):
                to = (2 * (pair % 2) + h) * XN + x
                start = 14 * (pair // 2)
                held[to, start : start + 14, :] = rows[pair, 56 * h + 14 * x : 56 * h + 14 * x + 14, :]
    for to in range(YN * XN):
        out[to] = held[to].astype(BF)


def pillar_body(
    got,
    low_far,
    high_far,
    direct,
    index_far,
    out,
    grad_fine_far,
    low,
    high,
    index,
    grad_fine,
    rows,
    sems,
):
    copies = fetch(sems, (index_far, index), (low_far, low), (high_far, high))
    total = got[0].astype(F32)
    for i in range(1, YN * XN):
        total = total + got[i].astype(F32)
    rows[:112, :] = total
    rows[112:, :] = jnp.zeros((16, WIDTH), F32)
    for z in range(ZN):
        out[z] = rows[14 * z : 14 * z + 16, :].astype(BF)
    for copy in copies:
        copy.wait()
    row = jnp.concatenate([piece(index, 0, 128), piece(index, 128, 64)], axis=1)
    total = direct[...] + dot(down(row[:, :RIM], NODES), low[...])
    total = total + dot(down(row[:, RIM:], NODES), high[...])
    grad_fine[...] = total.astype(BF)
    copy = pltpu.make_async_copy(grad_fine, grad_fine_far, sems.at[3])
    copy.start()
    copy.wait()


def last_body(got, out):
    total = got[0].astype(F32)
    for z in range(1, ZN):
        total = total + got[z].astype(F32)
    for r in range(TALL):
        for j in range(WIDTH // 128):
            here = pl.ds(WIDTH * r + 128 * j, 128)
            out[here] = total[r : r + 1, 128 * j : 128 * (j + 1)].reshape(128)


def on_device(
    fine_latent,
    mid_latent,
    send_index,
    edge_src,
    edge_dst,
    edge_count,
    up_row,
    up_node,
    w_src,
    w_dst,
    w_msg,
    w_node,
    w_mid,
    cot_fine,
    cot_mid,
):
    place_at = (lax.axis_index("row") % PLANE).astype(jnp.int32).reshape(1)
    dest = up_row.reshape(1, NODES)
    ahead = [(i, (i + 1) % 256) for i in range(256)]
    behind = [(j, i) for i, j in ahead]
    line = lambda n: pltpu.VMEM((n,), jnp.int32)
    hold = lambda *shape: pltpu.VMEM(shape, BF)
    wide = lambda *shape: pltpu.VMEM(shape, F32)
    rim, fine, mid = bf(RIM, WIDTH), bf(NODES, WIDTH), bf(MIDS, WIDTH)

    low, high = run(
        send_body,
        (rim, rim),
        (send_index, fine_latent),
        "hh>vv",
        (line(2 * RIM), hold(NODES, WIDTH)),
        copies=2,
        mib=60,
    )
    lower = lax.ppermute(high, BOTH, ahead)
    upper = lax.ppermute(low, BOTH, behind)
    near, mine, spot = run(
        local_body,
        (fine, fine, i32(1, NODES)),
        (dest, fine_latent, w_src, w_dst),
        "hhhh>vvv",
        (pltpu.VMEM((1, NODES), jnp.int32), hold(NODES, WIDTH), hold(WIDTH, WIDTH))
        + (hold(WIDTH, WIDTH),),
        copies=4,
        mib=60,
        flops=4 * NODES * WIDTH * WIDTH,
    )
    dma = pltpu.SemaphoreType.DMA
    fine_out, node_slope, edge_slope, gathered, aggregate, rims_in, *sent = run(
        forward_body,
        (fine, f32(NODES, WIDTH), bf(EDGES, WIDTH), fine, fine, bf(2 * RIM, WIDTH)) + PLANE * (bf(CARRY, WIDTH),),
        (edge_count, place_at, edge_src, edge_dst, near, mine, w_src, lower, upper, w_msg, w_node)
        + (fine_latent, spot, up_node),
        "ss" + 12 * "h" + ">" + 14 * "h",
        (line(EDGES), line(EDGES), hold(NODES, WIDTH), hold(WIDTH, WIDTH), hold(RIM, WIDTH))
        + (hold(RIM, WIDTH), hold(WIDTH, WIDTH), hold(2 * WIDTH, WIDTH), hold(NODES, WIDTH))
        + (pltpu.VMEM((1, NODES), jnp.int32), line(NODES), hold(NODES, WIDTH))
        + (hold(PLANE, CARRY, WIDTH), wide(NODES, WIDTH), hold(EDGES, WIDTH))
        + (hold(NODES, WIDTH), hold(NODES, WIDTH), hold(ENDS, WIDTH), hold(EDGES, ENDS))
        + (dma((12,)), dma((17,))),
        mib=60,
        flops=4 * 10**9,
    )
    got = [sent[0]]
    for (dy, dc), block in zip(PEERS[1:], sent[1:]):
        got.append(lax.ppermute(block, BOTH, shift(dy=dy, dc=dc)))
    sums, owner = run(sum_body, (bf(ZN, MIDS, WIDTH), i32(PLANE, 128)), got, 8 * "v" + ">vv")
    got = lax.all_to_all(sums, "row", 0, 0, axis_index_groups=PILLARS)
    spread, up_agg, mid_back, mid_out, grad_mid = run(
        mid_body,
        (bf(ZN, MIDS, WIDTH), mid, mid, mid, mid),
        (got, mid_latent, cot_mid, w_mid),
        "vhhh>vvvhh",
        (hold(MIDS, WIDTH), hold(MIDS, WIDTH), hold(2 * WIDTH, WIDTH))
        + 2 * (hold(MIDS, WIDTH),),
        copies=5,
    )
    got = lax.all_to_all(spread, "row", 0, 0, axis_index_groups=PILLARS)
    blocks = run(spread_body, PLANE * (bf(SLOTS, WIDTH),), (owner, got), "vv>" + 8 * "v")
    back = [blocks[0]]
    for (dy, dc), block in zip(PEERS[1:], blocks[1:]):
        back.append(lax.ppermute(block, BOTH, shift(dy=-dy, dc=-dc)))
    far = (cot_fine, node_slope, w_node, w_msg, edge_dst, gathered, fine_latent, aggregate)
    far += (mid_latent, edge_src, edge_slope, rims_in, w_src, w_dst)
    direct, low, high, keep, send = run(
        backward_body,
        (f32(NODES, WIDTH), rim, rim, bf(1792, WIDTH), bf(1792, WIDTH)),
        (edge_count, place_at, spot, up_agg, mid_back, *far, *back),
        "ss" + (3 + len(far) + PLANE) * "v" + ">vvvvv",
        (hold(NODES, WIDTH), hold(NODES, WIDTH), hold(NODES, WIDTH), hold(EXT + NODES, WIDTH))
        + (hold(EDGES, NODES), wide(EXT + NODES, WIDTH), wide(3584, WIDTH)),
        room=17_000_000,
        flops=5 * 10**9,
    )
    from_low = lax.ppermute(high, BOTH, ahead)
    from_high = lax.ppermute(low, BOTH, behind)
    got = lax.ppermute(send, BOTH, shift(dc=1))
    sheet = YN * XN
    (part,) = run(
        sheet_body,
        (bf(sheet, 112, WIDTH),),
        (keep, got),
        "vv>v",
        (wide(2 * ZN, 112, WIDTH), wide(sheet, 112, WIDTH)),
        mib=24,
    )
    part, from_low, from_high = lax.optimization_barrier((part, from_low, from_high))
    part = lax.all_to_all(part, BOTH, 0, 0, axis_index_groups=SHEETS)
    part, grad_fine = run(
        pillar_body,
        (bf(ZN, HELD, WIDTH), fine),
        (part, from_low, from_high, direct, send_index),
        "vhhvh>vh",
        (hold(RIM, WIDTH), hold(RIM, WIDTH), line(2 * RIM))
        + (hold(NODES, WIDTH), wide(128, WIDTH)),
        copies=4,
        mib=24,
    )
    part = lax.all_to_all(part, "row", 0, 0, axis_index_groups=PILLARS)
    (weight_grads,) = run(last_body, (f32(TALL * WIDTH),), (part,), "v>v")
    return fine_out, mid_out, grad_fine, grad_mid, weight_grads


def solution(mesh):
    rows, line = P(BOTH, None), P(BOTH)
    return jax.shard_map(
        on_device,
        mesh=mesh,
        in_specs=(rows, rows, line, line, line, line, rows, line)
        + (P(),) * 5
        + (rows, rows),
        out_specs=(rows, rows, rows, rows, line),
        check_vma=False,
    )
```

```python
import jax
import jax.numpy as jnp
from jax import lax
from jax.experimental import pallas as pl
from jax.experimental.pallas import tpu as pltpu
from jax.sharding import PartitionSpec as P

BF = jnp.bfloat16
F32 = jnp.float32
BOTH = ("row", "col")
CAP = 12
ZN, YN, CN, XN = 8, 4, 2, 4
PLANE = YN * CN
NODES, RIM, EXT, MIDS, WIDTH, EDGES = 384, 96, 576, 32, 512, 2304
SLOTS = ZN * CAP
CARRY = 112
STEP = 768
DST = 640
ENDS = DST + NODES
TALL = 14
HELD = 16
VMEM = 57_000_000


def place(z, y, c, x):
    return ((z * YN + y) * CN + c) * XN + x


def shift(dz=0, dy=0, dc=0, dx=0):
    return [
        (place(z, y, c, x), place((z + dz) % ZN, (y + dy) % YN, (c + dc) % CN, (x + dx) % XN))
        for z in range(ZN)
        for y in range(YN)
        for c in range(CN)
        for x in range(XN)
    ]


PLANES = [[z * PLANE + i for i in range(PLANE)] for z in range(ZN)]
PILLARS = [[z * PLANE + i for z in range(ZN)] for i in range(PLANE)]
SHEETS = [
    [place(z, y, c, x) for y in range(YN) for x in range(XN)] for z in range(ZN) for c in range(CN)
]


PEERS = ((0, 0), (2, 0), (2, 1), (1, 0), (1, 1), (3, 0), (3, 1), (0, 1))


def peer(me, dy, dc):
    return (((me >> 1) + dy) & (YN - 1)) * CN + ((me & 1) ^ dc)


def dot(a, b):
    return jnp.dot(a, b, preferred_element_type=F32)


def dot_t(a, b):
    return lax.dot_general(a, b, (((0,), (0,)), ((), ())), preferred_element_type=F32)


def dot_nt(a, b):
    return lax.dot_general(a, b, (((1,), (1,)), ((), ())), preferred_element_type=F32)


def iota(shape, axis):
    return lax.broadcasted_iota(jnp.int32, shape, axis)


def ones(mask):
    return jnp.where(mask, 1.0, 0.0).astype(BF)


def across(row):
    return jnp.transpose(jnp.broadcast_to(row, (128, 128)))


def down(row, count, start=0):
    return ones(iota((count, row.shape[1]), 0) + start == row)


def silu_pair(u):
    s = 0.5 * jnp.tanh(0.5 * u) + 0.5
    return u * s, s * (1.0 + u * (1.0 - s))


def bf(*shape):
    return jax.ShapeDtypeStruct(shape, BF)


def f32(*shape):
    return jax.ShapeDtypeStruct(shape, F32)


def i32(*shape):
    return jax.ShapeDtypeStruct(shape, jnp.int32)


def run(body, outs, args, kinds, scratch=(), copies=0, mib=16, room=0, flops=0):
    spaces = {"s": pltpu.SMEM, "v": pltpu.VMEM, "h": pltpu.HBM}
    moved = sum(a.size * a.dtype.itemsize for a in list(args) + list(outs))
    took, gave = kinds.split(">")
    scratch = list(scratch)
    limit = VMEM - room if room else mib << 20
    if copies:
        scratch.append(pltpu.SemaphoreType.DMA((copies,)))
    return pl.pallas_call(
        body,
        out_shape=list(outs),
        in_specs=[pl.BlockSpec(memory_space=spaces[k]) for k in took],
        out_specs=[pl.BlockSpec(memory_space=spaces[k]) for k in gave],
        scratch_shapes=scratch,
        compiler_params=pltpu.CompilerParams(vmem_limit_bytes=limit),
        cost_estimate=pl.CostEstimate(flops=flops, bytes_accessed=moved, transcendentals=0),
    )(*args)


def fetch(sems, *pairs):
    copies = [pltpu.make_async_copy(a, b, sems.at[i]) for i, (a, b) in enumerate(pairs)]
    for copy in copies:
        copy.start()
    return copies


def piece(line, start, size):
    return line[pl.ds(start, size)].reshape(1, size)


def send_body(index_far, latent_far, low, high, index, latent, sems):
    for copy in fetch(sems, (index_far, index), (latent_far, latent)):
        copy.wait()
    row = jnp.concatenate([piece(index, 0, 128), piece(index, 128, 64)], axis=1)
    rows = dot_t(down(row, NODES), latent[...]).astype(BF)
    low[...] = rows[:RIM]
    high[...] = rows[RIM:]


def local_body(
    dest_far, latent_far, w_src_far, w_dst_far, near, mine, spot, dest, latent, w_src, w_dst, sems
):
    copies = fetch(
        sems, (dest_far, dest), (latent_far, latent), (w_src_far, w_src), (w_dst_far, w_dst)
    )
    copies[0].wait()
    for j in range(NODES // 128):
        row = dest[:, 128 * j : 128 * (j + 1)]
        rank = jnp.zeros((1, 128), F32)
        for b in range(j + 1):
            same = across(dest[:, 128 * b : 128 * (b + 1)]) == row
            if b == j:
                same = same & (iota((128, 128), 0) < iota((128, 128), 1))
            rank = rank + jnp.sum(jnp.where(same, 1.0, 0.0), axis=0, keepdims=True)
        spot[:, 128 * j : 128 * (j + 1)] = (
            (row & (PLANE - 1)) * SLOTS + (row >> 3) * CAP + rank.astype(jnp.int32)
        )
    for copy in copies[1:]:
        copy.wait()
    near[...] = dot(latent[...], w_src[...]).astype(BF)
    mine[...] = dot(latent[...], w_dst[...]).astype(BF)


def live_row(row, count, start):
    return jnp.where(iota(row.shape, 1) + start < count, row, -1)


def forward_body(
    count,
    place_at,
    src_far,
    dst_far,
    near_far,
    mine_far,
    w_src_far,
    lower_far,
    upper_far,
    w_msg_far,
    w_node_far,
    latent_far,
    spot_far,
    node_far,
    fine_out_far,
    node_slope_far,
    slope_far,
    gathered_far,
    aggregate_far,
    rims_far,
    *rest,
):
    sent_far, rest = rest[:PLANE], rest[PLANE:]
    src, dst, mine, w_src, lower, upper, w_msg, w_node, latent, spot, node = rest[:11]
    fine_out, sent, node_slope, edge_slope, gathered, aggregate = rest[11:17]
    table, ends, sems, out_sems = rest[17:]
    near = table.at[:NODES, :]
    copies = fetch(
        sems,
        (src_far, src),
        (dst_far, dst),
        (w_src_far, w_src),
        (lower_far, lower),
        (upper_far, upper),
        (near_far, near),
        (mine_far, mine),
        (w_msg_far, w_msg),
        (w_node_far, w_node),
        (latent_far, latent),
        (spot_far, spot),
        (node_far, node),
    )
    stores = []

    def store(here, there):
        stores.append(pltpu.make_async_copy(here, there, out_sems.at[len(stores)]))
        stores[-1].start()

    table[EXT:DST, :] = jnp.zeros((DST - EXT, WIDTH), BF)
    for copy in copies[:2]:
        copy.wait()
    lane = iota((128, 128), 1)
    total = jnp.zeros((NODES, WIDTH), F32)
    for start in range(0, EDGES, STEP):
        for at in range(start, start + STEP, 128):
            source, target = across(piece(src, at, 128)), across(piece(dst, at, 128))
            for j in range(0, DST, 128):
                ends[at : at + 128, j : j + 128] = ones(source == lane + j)
            for j in range(0, NODES, 128):
                ends[at : at + 128, DST + j : DST + j + 128] = ones(target == lane + j)
        if start == 0:
            for copy in copies[2:7]:
                copy.wait()
            store(lower, rims_far.at[pl.ds(0, RIM)])
            store(upper, rims_far.at[pl.ds(RIM, RIM)])
            table[DST:, :] = mine[...]
            table[NODES : NODES + RIM, :] = dot(lower[...], w_src[...]).astype(BF)
            table[NODES + RIM : EXT, :] = dot(upper[...], w_src[...]).astype(BF)
        act, slope = silu_pair(dot(ends[start : start + STEP, :], table[...]))
        here = pl.ds(start, STEP)
        edge_slope[here, :] = slope.astype(BF)
        store(edge_slope.at[here, :], slope_far.at[here, :])
        row = live_row(piece(dst, start, STEP), count[0], start)
        total = total + dot(down(row, NODES), act.astype(BF))
    gathered[...] = total.astype(BF)
    store(gathered, gathered_far)
    for copy in copies[7:]:
        copy.wait()
    aggregate[...] = dot(gathered[...], w_msg[...]).astype(BF)
    store(aggregate, aggregate_far)
    update = dot(latent[...], w_node[:WIDTH, :]) + dot(aggregate[...], w_node[WIDTH:, :])
    lift, slope = silu_pair(update)
    node_slope[...] = slope
    store(node_slope, node_slope_far)
    fine_out[...] = (latent[...].astype(F32) + lift).astype(BF)
    store(fine_out, fine_out_far)
    names = jnp.broadcast_to((piece(node, 0, NODES) + 1).astype(F32), (16, NODES)).astype(BF)
    for i, (dy, dc) in enumerate(PEERS):
        offset = spot[...] - peer(place_at[0], dy, dc) * SLOTS
        to_slot = ones((iota((128, NODES), 0) == offset) & (offset < SLOTS))
        sent[i] = dot(to_slot[:CARRY], fine_out[...]).astype(BF)
        sent[i, SLOTS:CARRY, :128] = dot_nt(names, to_slot).astype(BF)
        store(sent.at[i], sent_far[i])
    for copy in stores:
        copy.wait()


def sum_body(*refs):
    got, (sums, owner) = refs[:PLANE], refs[PLANE:]
    total = jnp.zeros((ZN * MIDS, WIDTH), F32)
    level = iota((1, 128), 1)
    base = jnp.zeros((1, 128), jnp.int32)
    for z in range(1, ZN):
        base = base + jnp.where(level >= z * CAP, MIDS, 0)
    for i in range(PLANE):
        name = got[i][SLOTS:CARRY, :128][:1].astype(F32).astype(jnp.int32)
        name = jnp.where((name > 0) & (level < SLOTS), name - 1 + base, -1)
        owner[i : i + 1, :] = name
        total = total + dot(down(name, ZN * MIDS)[:, :CARRY], got[i][...])
    for z in range(ZN):
        sums[z] = total[z * MIDS : (z + 1) * MIDS].astype(BF)


def mid_body(
    got,
    latent_far,
    cot_far,
    w_mid_far,
    spread,
    up_agg,
    mid_back,
    mid_out_far,
    grad_mid_far,
    latent,
    cot,
    w_mid,
    mid_out,
    grad_mid,
    sems,
):
    copies = fetch(sems, (latent_far, latent), (cot_far, cot), (w_mid_far, w_mid))
    total = got[0].astype(F32)
    for z in range(1, ZN):
        total = total + got[z].astype(F32)
    agg = (0.25 * total).astype(BF)
    up_agg[...] = agg
    for copy in copies:
        copy.wait()
    update = dot(latent[...], w_mid[:WIDTH, :]) + dot(agg, w_mid[WIDTH:, :])
    lift, slope = silu_pair(update)
    mid_out[...] = (latent[...].astype(F32) + lift).astype(BF)
    back = (cot[...].astype(F32) * slope).astype(BF)
    mid_back[...] = back
    stores = [
        pltpu.make_async_copy(mid_out, mid_out_far, sems.at[3]),
        pltpu.make_async_copy(grad_mid, grad_mid_far, sems.at[4]),
    ]
    stores[0].start()
    grad = dot_nt(back, w_mid[:WIDTH, :]).astype(BF).astype(F32)
    grad_mid[...] = (cot[...].astype(F32) + grad).astype(BF)
    stores[1].start()
    grad = dot_nt(back, w_mid[WIDTH:, :]).astype(BF).astype(F32)
    grad = (0.25 * grad).astype(BF)
    for z in range(ZN):
        spread[z] = grad
    for copy in stores:
        copy.wait()


def spread_body(owner, got, *back):
    rows = jnp.concatenate([got[z] for z in range(ZN)], axis=0)
    for i in range(PLANE):
        back[i][...] = dot_t(down(owner[i : i + 1, :], ZN * MIDS), rows)[:SLOTS].astype(BF)


def part_cores(mine, flat, first, pairs, keep, send):
    for pair in range(first, first + pairs):
        even, odd = [
            jnp.concatenate(
                [flat[pl.ds(224 * pair + 112 * h + 56 * c, 56), :] for h in range(2)], axis=0
            )
            for c in range(CN)
        ]
        keep[112 * pair : 112 * (pair + 1), :] = jnp.where(mine == 0, even, odd).astype(BF)
        send[112 * pair : 112 * (pair + 1), :] = jnp.where(mine == 0, odd, even).astype(BF)


def backward_body(count, place_at, *refs):
    spot, cot, node_slope, w_node, w_msg, dst, src, edge_slope, w_src, w_dst = refs[:10]
    back, refs = refs[10 : 10 + PLANE], refs[10 + PLANE :]
    direct, low, high, node_back, grad_agg, grad_ends = refs[:6]
    grad_gathered, targets, total = refs[6:]
    up = jnp.zeros((NODES, WIDTH), F32)
    for i, (dy, dc) in enumerate(PEERS):
        offset = spot[...] - peer(place_at[0], dy, dc) * SLOTS
        up = up + dot_t(down(offset, SLOTS), back[i][...])
    cot_sum = (cot[...].astype(F32) + up).astype(BF).astype(F32)
    node_back[...] = (cot_sum * node_slope[...]).astype(BF)
    grad_agg[...] = dot_nt(node_back[...], w_node[WIDTH:, :]).astype(BF)
    grad_gathered[...] = dot_nt(grad_agg[...], w_msg[...]).astype(BF)
    direct[...] = cot_sum + dot_nt(node_back[...], w_node[:WIDTH, :]).astype(BF).astype(F32)
    lane = iota((128, 128), 1)
    for start in range(0, EDGES, STEP):
        for at in range(start, start + STEP, 128):
            target = across(piece(dst, at, 128))
            for j in range(0, NODES, 128):
                targets[at : at + 128, j : j + 128] = ones(target == lane + j)
        grad = dot(targets[start : start + STEP, :], grad_gathered[...])
        grad = (grad * edge_slope[start : start + STEP, :].astype(F32)).astype(BF)
        from_src = dot(down(live_row(piece(src, start, STEP), count[0], start), EXT), grad)
        from_dst = dot(down(live_row(piece(dst, start, STEP), count[0], start), NODES), grad)
        if start == 0:
            total[:EXT, :] = from_src
            total[EXT:, :] = from_dst
        else:
            total[:EXT, :] += from_src
            total[EXT:, :] += from_dst
    grad_ends[...] = total[...].astype(BF)
    rims = dot_nt(grad_ends[NODES:EXT, :], w_src[...]).astype(BF)
    low[...] = rims[:RIM]
    high[...] = rims[RIM:]
    grad = dot_nt(grad_ends[:NODES, :], w_src[...]) + dot_nt(grad_ends[EXT:, :], w_dst[...])
    direct[...] += grad


def weights_body(place_at, *refs):
    up_agg, mid_back, gathered, latent, aggregate, mid, rims_in = refs[:7]
    node_back, grad_agg, grad_ends, keep, send, flat = refs[7:]
    mine = place_at[0] & 1
    flat[1024:1536, :] = dot_t(gathered[...], grad_agg[...])
    flat[1536:2048, :] = dot_t(latent[...], node_back[...])
    flat[2048:2560, :] = dot_t(aggregate[...], node_back[...])
    flat[2560:3072, :] = dot_t(mid[...], mid_back[...])
    flat[3072:, :] = dot_t(up_agg[...], mid_back[...])
    part_cores(mine, flat, 5, 11, keep, send)
    grad = dot_t(rims_in[...], grad_ends[NODES:EXT, :])
    flat[:512, :] = grad + dot_t(latent[...], grad_ends[:NODES, :])
    flat[512:1024, :] = dot_t(latent[...], grad_ends[EXT:, :])
    part_cores(mine, flat, 0, 5, keep, send)


def sheet_body(keep, got, out, rows, held):
    for pair in range(2 * ZN):
        at = 112 * pair
        rows[pair] = keep[at : at + 112, :].astype(F32) + got[at : at + 112, :].astype(F32)
        for h in range(2):
            for x in range(XN):
                to = (2 * (pair % 2) + h) * XN + x
                start = 14 * (pair // 2)
                held[to, start : start + 14, :] = rows[pair, 56 * h + 14 * x : 56 * h + 14 * x + 14, :]
    for to in range(YN * XN):
        out[to] = held[to].astype(BF)


def pillar_body(got, out, rows):
    total = got[0].astype(F32)
    for i in range(1, YN * XN):
        total = total + got[i].astype(F32)
    rows[:112, :] = total
    rows[112:, :] = jnp.zeros((16, WIDTH), F32)
    for z in range(ZN):
        out[z] = rows[14 * z : 14 * z + 16, :].astype(BF)


def final_body(direct, low, high, index, grad_fine):
    row = jnp.concatenate([piece(index, 0, 128), piece(index, 128, 64)], axis=1)
    total = direct[...] + dot(down(row[:, :RIM], NODES), low[...])
    total = total + dot(down(row[:, RIM:], NODES), high[...])
    grad_fine[...] = total.astype(BF)


def last_body(got, out):
    total = got[0].astype(F32)
    for z in range(1, ZN):
        total = total + got[z].astype(F32)
    for r in range(TALL):
        for j in range(WIDTH // 128):
            here = pl.ds(WIDTH * r + 128 * j, 128)
            out[here] = total[r : r + 1, 128 * j : 128 * (j + 1)].reshape(128)


def on_device(
    fine_latent,
    mid_latent,
    send_index,
    edge_src,
    edge_dst,
    edge_count,
    up_row,
    up_node,
    w_src,
    w_dst,
    w_msg,
    w_node,
    w_mid,
    cot_fine,
    cot_mid,
):
    place_at = (lax.axis_index("row") % PLANE).astype(jnp.int32).reshape(1)
    dest = up_row.reshape(1, NODES)
    ahead = [(i, (i + 1) % 256) for i in range(256)]
    behind = [(j, i) for i, j in ahead]
    line = lambda n: pltpu.VMEM((n,), jnp.int32)
    hold = lambda *shape: pltpu.VMEM(shape, BF)
    wide = lambda *shape: pltpu.VMEM(shape, F32)
    rim, fine, mid = bf(RIM, WIDTH), bf(NODES, WIDTH), bf(MIDS, WIDTH)

    low, high = run(
        send_body,
        (rim, rim),
        (send_index, fine_latent),
        "hh>vv",
        (line(2 * RIM), hold(NODES, WIDTH)),
        copies=2,
        mib=60,
    )
    lower = lax.ppermute(high, BOTH, ahead)
    upper = lax.ppermute(low, BOTH, behind)
    near, mine, spot = run(
        local_body,
        (fine, fine, i32(1, NODES)),
        (dest, fine_latent, w_src, w_dst),
        "hhhh>vvv",
        (pltpu.VMEM((1, NODES), jnp.int32), hold(NODES, WIDTH), hold(WIDTH, WIDTH))
        + (hold(WIDTH, WIDTH),),
        copies=4,
        mib=60,
        flops=4 * NODES * WIDTH * WIDTH,
    )
    dma = pltpu.SemaphoreType.DMA
    fine_out, node_slope, edge_slope, gathered, aggregate, rims_in, *sent = run(
        forward_body,
        (fine, f32(NODES, WIDTH), bf(EDGES, WIDTH), fine, fine, bf(2 * RIM, WIDTH)) + PLANE * (bf(CARRY, WIDTH),),
        (edge_count, place_at, edge_src, edge_dst, near, mine, w_src, lower, upper, w_msg, w_node)
        + (fine_latent, spot, up_node),
        "ss" + 12 * "h" + ">" + 14 * "h",
        (line(EDGES), line(EDGES), hold(NODES, WIDTH), hold(WIDTH, WIDTH), hold(RIM, WIDTH))
        + (hold(RIM, WIDTH), hold(WIDTH, WIDTH), hold(2 * WIDTH, WIDTH), hold(NODES, WIDTH))
        + (pltpu.VMEM((1, NODES), jnp.int32), line(NODES), hold(NODES, WIDTH))
        + (hold(PLANE, CARRY, WIDTH), wide(NODES, WIDTH), hold(EDGES, WIDTH))
        + (hold(NODES, WIDTH), hold(NODES, WIDTH), hold(ENDS, WIDTH), hold(EDGES, ENDS))
        + (dma((12,)), dma((17,))),
        mib=60,
        flops=4 * 10**9,
    )
    got = [sent[0]]
    for (dy, dc), block in zip(PEERS[1:], sent[1:]):
        got.append(lax.ppermute(block, BOTH, shift(dy=dy, dc=dc)))
    sums, owner = run(sum_body, (bf(ZN, MIDS, WIDTH), i32(PLANE, 128)), got, 8 * "v" + ">vv")
    got = lax.all_to_all(sums, "row", 0, 0, axis_index_groups=PILLARS)
    spread, up_agg, mid_back, mid_out, grad_mid = run(
        mid_body,
        (bf(ZN, MIDS, WIDTH), mid, mid, mid, mid),
        (got, mid_latent, cot_mid, w_mid),
        "vhhh>vvvhh",
        (hold(MIDS, WIDTH), hold(MIDS, WIDTH), hold(2 * WIDTH, WIDTH))
        + 2 * (hold(MIDS, WIDTH),),
        copies=5,
    )
    got = lax.all_to_all(spread, "row", 0, 0, axis_index_groups=PILLARS)
    blocks = run(spread_body, PLANE * (bf(SLOTS, WIDTH),), (owner, got), "vv>" + 8 * "v")
    back = [blocks[0]]
    for (dy, dc), block in zip(PEERS[1:], blocks[1:]):
        back.append(lax.ppermute(block, BOTH, shift(dy=-dy, dc=-dc)))
    direct, low, high, node_back, grad_agg, grad_ends = run(
        backward_body,
        (f32(NODES, WIDTH), rim, rim, fine, fine, bf(EXT + NODES, WIDTH)),
        (edge_count, place_at, spot, cot_fine, node_slope, w_node, w_msg, edge_dst, edge_src)
        + (edge_slope, w_src, w_dst, *back),
        "ss" + 18 * "v" + ">" + 6 * "v",
        (hold(NODES, WIDTH), hold(EDGES, NODES), wide(EXT + NODES, WIDTH)),
        room=17_000_000,
        flops=4 * 10**9,
    )
    keep, send = run(
        weights_body,
        (bf(1792, WIDTH), bf(1792, WIDTH)),
        (place_at, up_agg, mid_back, gathered, fine_latent, aggregate, mid_latent, rims_in)
        + (node_back, grad_agg, grad_ends),
        "s" + 10 * "v" + ">vv",
        (wide(3584, WIDTH),),
        room=17_000_000,
        flops=2 * 10**9,
    )
    got = lax.ppermute(send, BOTH, shift(dc=1))
    sheet = YN * XN
    (part,) = run(
        sheet_body,
        (bf(sheet, 112, WIDTH),),
        (keep, got),
        "vv>v",
        (wide(2 * ZN, 112, WIDTH), wide(sheet, 112, WIDTH)),
        mib=24,
    )
    part = lax.all_to_all(part, BOTH, 0, 0, axis_index_groups=SHEETS)
    part, low, high = lax.optimization_barrier((part, low, high))
    from_low = lax.ppermute(high, BOTH, ahead)
    from_high = lax.ppermute(low, BOTH, behind)
    (part,) = run(pillar_body, (bf(ZN, HELD, WIDTH),), (part,), "v>v", (wide(128, WIDTH),))
    part = lax.all_to_all(part, "row", 0, 0, axis_index_groups=PILLARS)
    (grad_fine,) = run(
        final_body,
        (fine,),
        (direct, from_low, from_high, send_index),
        "vvvv>v",
        flops=2 * 10**8,
    )
    (weight_grads,) = run(last_body, (f32(TALL * WIDTH),), (part,), "v>v")
    return fine_out, mid_out, grad_fine, grad_mid, weight_grads


def solution(mesh):
    rows, line = P(BOTH, None), P(BOTH)
    return jax.shard_map(
        on_device,
        mesh=mesh,
        in_specs=(rows, rows, line, line, line, line, rows, line)
        + (P(),) * 5
        + (rows, rows),
        out_specs=(rows, rows, rows, rows, line),
        check_vma=False,
    )
```
